256 devices in a mesh: seq: 32 (over y, x, core), head: 8 (over z).
Axes of the slice: x: 4, y: 4, z: 8, core: 2. Of those that a mesh axis runs over, the one named last changes fastest.
Arguments:
- queries: bfloat16 [16384, 4096], P('seq', 'head'), may hold values from -6 to 6
- keys: bfloat16 [16384, 4096], P('seq', 'head'), may hold values from -6 to 6
- values: bfloat16 [16384, 4096], P('seq', 'head'), may hold values from -48 to 48
- gate_logits: bfloat16 [16384, 4096], P('seq', 'head'), may hold values from -8 to 8
- out_weight: bfloat16 [4096, 6144], P('head'), may hold values from -0.125 to 0.125
Outputs:
- layer_out: bfloat16 [16384, 6144], P('seq', 'head')
The draws below stay inside these ranges and needn't reach their ends.
All inputs are finite; a program needn't handle non-finite values.
Results may differ from the reference program's by a relative error of at most 0.02.
Values may be sent and summed in bfloat16 or wider, within the bound.
A program may use at most 64 MiB of HBM per device.

```python
import jax
import jax.numpy as jnp
from jax import lax

D = 6144
HEADS = 32
HEAD_DIM = 128
BLOCK = 512
TOKENS = 16384
HD = 4096
N_HEAD = 8


def draw_values(key, part):
    first_key, second_key = jax.random.split(key, 2)
    columns = HEADS * HEAD_DIM
    head_number = (jnp.arange(columns) // HEAD_DIM).astype(jnp.float32)
    ramp = 3.0 ** (head_number / max(HEADS - 1, 1))
    column_gain = jax.random.uniform(second_key, (columns,), jnp.float32, 0.6, 1.6)
    base = jnp.clip(jax.random.normal(first_key, (TOKENS, columns), jnp.float32), -6.0, 6.0)
    return (base * ramp[None, :] * column_gain[None, :]).astype(jnp.bfloat16)


def spiked(entries, stream_key, source, target, blocks, factor):
    def block_of(axis_at):
        return (jnp.arange(entries.shape[axis_at]) // (entries.shape[axis_at] // blocks)).reshape((-1,) + (1,) * (entries.ndim - 1 - axis_at))

    first = jax.random.permutation(stream_key, blocks)[block_of(target)]
    far = (block_of(target) + blocks // 2) % blocks
    return jnp.where((block_of(source) == first) | (block_of(source) == far), factor * entries, entries)


def steps_of(stream_key, extent, pieces, smallest, top_value):
    loudness = 1.0
    for dim, blocks in pieces:
        draws = jax.random.uniform(jax.random.fold_in(jax.random.fold_in(stream_key, 6), dim), (blocks,), jnp.float32, smallest / len(pieces), top_value / len(pieces))
        loudness = loudness * jnp.repeat(jnp.exp(draws), extent[dim] // blocks).reshape((-1,) + (1,) * (len(extent) - 1 - dim))
    return loudness


def centred(stream_key, shape, width, bound, shards=(), kind=jnp.bfloat16):
    values = jax.random.normal(stream_key, shape, jnp.float32) * width
    if len(shards) > 0:
        values = steps_of(stream_key, shape, shards, -0.22, 0.18) * values
    return jnp.clip(values, min=-bound, max=bound).astype(kind)


def noise_with(own_key, extent, deviation, reach, shards, heavy, held_as=jnp.bfloat16):
    array = deviation * jax.random.normal(own_key, extent, jnp.float32)
    if shards:
        array = array * steps_of(own_key, extent, shards, -0.22, 0.18)
    return jnp.clip(spiked(array, jax.random.fold_in(own_key, 3), *heavy), -reach, reach).astype(held_as)


def setup_inputs(seed: int = 0) -> dict:
    splits = jax.random.split(jax.random.key(seed), 6)
    queries = centred(splits[0], (TOKENS, HD), 1.0, 6.0, ((0, 32), (1, 8)))
    keys = centred(splits[1], (TOKENS, HD), 1.0, 6.0, ((0, 32), (1, 8)))
    values = draw_values(jax.random.fold_in(splits[5], 71), 0)
    gate_logits = centred(splits[3], (TOKENS, HD), 1.5, 8.0, ((0, 32), (1, 8)))
    out_weight = noise_with(splits[4], (HD, D), HD ** -0.5, 0.125, ((0, 8),), (0, 1, 8, 2.0))
    return dict(queries=queries, keys=keys, values=values, gate_logits=gate_logits, out_weight=out_weight)


def activate(raw_input):
    return jax.nn.silu(raw_input.astype(jnp.float32)).astype(jnp.bfloat16)

def reference(queries, keys, values, gate_logits, out_weight):
    block_count = TOKENS // BLOCK
    active_q = activate(queries).reshape(block_count, BLOCK, HEADS, HEAD_DIM)
    active_k = activate(keys).reshape(block_count, BLOCK, HEADS, HEAD_DIM)
    active_v = activate(values).reshape(block_count, BLOCK, HEADS, HEAD_DIM)
    causal_mask = jnp.tril(jnp.ones((BLOCK, BLOCK), jnp.float32))

    def advance(carried, blocks):
        query_blk, key_blk, value_blk = blocks
        query_f = query_blk.astype(jnp.float32)
        key_f = key_blk.astype(jnp.float32)
        value_f = value_blk.astype(jnp.float32)
        scores = (jnp.einsum('thd,shd->hts', query_f, key_f) * causal_mask).astype(jnp.bfloat16)
        within_block = jnp.einsum('hts,shd->thd', scores.astype(jnp.float32), value_f)
        state_bf = carried.astype(jnp.bfloat16).astype(jnp.float32)
        from_state = jnp.einsum('thd,hde->the', query_f, state_bf)
        updated = carried + jnp.einsum('shd,she->hde', key_f, value_f)
        return (updated, within_block + from_state)
    initial = jnp.zeros((HEADS, HEAD_DIM, HEAD_DIM), jnp.float32)
    final_state, attended = lax.scan(advance, initial, (active_q, active_k, active_v))
    attended = attended.reshape(TOKENS, HD)
    mean_square = lax.optimization_barrier(jnp.mean(attended * attended, axis=-1, keepdims=True))
    gate = jax.nn.sigmoid(gate_logits.astype(jnp.float32))
    normed = (attended * lax.rsqrt(mean_square + 1e-06) * gate).astype(jnp.bfloat16)
    group_width = HD // N_HEAD
    normed_groups = normed.reshape(TOKENS, N_HEAD, group_width).transpose(1, 0, 2)
    weight_groups = out_weight.reshape(N_HEAD, group_width, D)

    def accumulate(total, group):
        normed_part, weight_part = group
        partial_sum = jnp.dot(normed_part, weight_part, preferred_element_type=jnp.float32)
        return (total + partial_sum.astype(jnp.bfloat16).astype(jnp.float32), None)
    total, unused = lax.scan(accumulate, jnp.zeros((TOKENS, D), jnp.float32), (normed_groups, weight_groups))
    return total.astype(jnp.bfloat16)
```

```python
import functools

import jax
import jax.numpy as jnp
from jax import lax
from jax.experimental import pallas as pl
from jax.experimental.pallas import tpu as pltpu
from jax.sharding import PartitionSpec as P

HEADS = 32
HEAD_DIM = 128
F32 = jnp.float32
BF16 = jnp.bfloat16
MESH = pl.DeviceIdType.MESH

NX = 4
NZ = 8
ROWS = 512
FEAT = 512
OUT = 768
CHUNK = 128
NCHUNK = ROWS // CHUNK
HALF = OUT // 2


def sigmoid(value):
    return 0.5 + 0.5 * jnp.tanh(0.5 * value)


def silu(raw):
    value = raw.astype(F32)
    return (value * sigmoid(value)).astype(BF16)


def contract(lhs, rhs, lhs_dim, rhs_dim):
    return lax.dot_general(
        lhs, rhs, (((lhs_dim,), (rhs_dim,)), ((), ())), preferred_element_type=F32
    )


def kernel(
    q_hbm, k_hbm, v_hbm, g_hbm, w_hbm, out_ref,
    q_in, k_in, v_in, g_in, aq, ak, av, within, gate,
    s_full, s_bf, sib, tot_bf, arr_a, pay, arr_b, back, state,
    gathered, weight, acc, ss_own, ss_all,
    load_sem, z_send, z_recv, p_send, p_recv, a_send, a_recv, b_send, b_recv,
    ss_send, ss_recv, r_send, r_recv, l_send, l_recv,
    wa_send, wa_recv, wb_send, wb_recv, ws_send, ws_recv,
):
    seq = lax.axis_index("seq")
    z = lax.axis_index("head")
    c = lax.rem(seq, 2)
    x = lax.rem(lax.div(seq, 2), NX)
    y = lax.div(seq, 2 * NX)
    a = x * (1 - c) + y * c
    b = y * (1 - c) + x * c

    def on_plane(a2, b2):
        x2 = a2 * (1 - c) + b2 * c
        y2 = b2 * (1 - c) + a2 * c
        return ((y2 * NX + x2) * 2 + c, z)

    def a_peer(step):
        return on_plane(lax.rem(a + step, NX), b)

    def b_peer(step):
        return on_plane(a, lax.rem(b + step, NX))

    def z_peer(step):
        return (seq, lax.rem(z + step, NZ))

    sibling = (seq + 1 - 2 * c, z)

    def remote(src, dst, send_sem, recv_sem, device):
        return pltpu.make_async_remote_copy(
            src_ref=src, dst_ref=dst, send_sem=send_sem, recv_sem=recv_sem,
            device_id=device, device_id_type=MESH,
        )

    barrier = pltpu.get_barrier_semaphore()
    partners = (
        [sibling]
        + [a_peer(step) for step in range(1, NX)]
        + [b_peer(step) for step in range(1, NX)]
        + [z_peer(step) for step in range(1, NZ)]
    )
    for partner in partners:
        pl.semaphore_signal(barrier, inc=1, device_id=partner, device_id_type=MESH)

    def load(src, dst, index):
        copy = pltpu.make_async_copy(src, dst, load_sem.at[index])
        copy.start()
        return copy

    load_k = load(k_hbm, k_in, 0)
    load_v = load(v_hbm, v_in, 1)
    load_q = load(q_hbm, q_in, 2)
    load_g = load(g_hbm, g_in, 3)
    own_columns = pl.ds(pl.multiple_of(z * OUT, 128), OUT)
    load_w = load(w_hbm.at[:, own_columns], weight.at[0], 4)

    def head(h):
        return slice(h * HEAD_DIM, (h + 1) * HEAD_DIM)

    load_k.wait()
    load_v.wait()
    for h in range(4):
        ak[:, head(h)] = silu(k_in[:, head(h)])
        av[:, head(h)] = silu(v_in[:, head(h)])
        outer = contract(ak[:, head(h)], av[:, head(h)], 0, 0)
        s_full[h] = outer
        s_bf[h] = outer.astype(BF16)

    pl.semaphore_wait(barrier, len(partners))

    mine = pl.ds(c * 2, 2)
    first = remote(
        s_bf.at[pl.ds((1 - c) * 2, 2)], sib, p_send.at[0], p_recv.at[0], sibling
    )
    first.start()

    share = pl.multiple_of(c * 256 + b * 64 + a * 16, 16)
    weight_z = []
    for step in range(1, NZ):
        columns = pl.ds(pl.multiple_of(lax.rem(z + step, NZ) * OUT, 128), OUT)
        copy = remote(
            w_hbm.at[pl.ds(share, 16), columns],
            weight.at[NZ - step, pl.ds(share, 16)],
            z_send.at[step - 1], z_recv.at[step - 1], z_peer(step),
        )
        copy.start()
        weight_z.append(copy)

    load_q.wait()
    for h in range(4):
        aq[:, head(h)] = silu(q_in[:, head(h)])

    first.wait_recv()
    total = s_full[mine] + sib[...].astype(F32)
    tot_bf[...] = total.astype(BF16)

    phase_a = []
    for step in range(1, NX):
        copy = remote(
            tot_bf, arr_a.at[step - 1], a_send.at[step - 1], a_recv.at[step - 1], a_peer(step)
        )
        copy.start()
        phase_a.append(copy)

    half = ROWS // 2
    row_id = lax.broadcasted_iota(jnp.int32, (half, half), 0)
    col_id = lax.broadcasted_iota(jnp.int32, (half, half), 1)
    causal = row_id >= col_id

    def attend_block(h):
        for part in range(2):
            rows = slice(part * half, (part + 1) * half)
            qh = aq[rows, head(h)]
            diag = contract(qh, ak[rows, head(h)], 1, 1)
            diag = jnp.where(causal, diag, 0.0).astype(BF16)
            result = contract(diag, av[rows, head(h)], 1, 0)
            if part == 1:
                low = contract(qh, ak[0:half, head(h)], 1, 1).astype(BF16)
                result = result + contract(low, av[0:half, head(h)], 1, 0)
            within[rows, head(h)] = result

    attend_block(0)
    attend_block(1)

    for copy in phase_a:
        copy.wait_recv()
    total = s_full[mine] + sib[...].astype(F32)
    low_sum = jnp.zeros((2, HEAD_DIM, HEAD_DIM), F32)
    all_sum = total
    for step in range(1, NX):
        term = arr_a[step - 1].astype(F32)
        low_sum = low_sum + term * jnp.where(a >= step, 1.0, 0.0).astype(F32)
        all_sum = all_sum + term
    core0 = jnp.where(c == 0, 1.0, 0.0).astype(F32)
    core1 = 1.0 - core0
    pay[0] = (core0 * all_sum + core1 * (low_sum + total)).astype(BF16)
    pay[1] = (core1 * low_sum).astype(BF16)

    phase_b = []
    for step in range(1, NX):
        copy = remote(
            pay.at[lax.div(b + step, NX)], arr_b.at[step - 1],
            b_send.at[step - 1], b_recv.at[step - 1], b_peer(step),
        )
        copy.start()
        phase_b.append(copy)

    attend_block(2)
    attend_block(3)
    load_g.wait()
    for h in range(4):
        gate[:, head(h)] = sigmoid(g_in[:, head(h)].astype(F32))

    low_sum = jnp.zeros((2, HEAD_DIM, HEAD_DIM), F32)
    for step in range(1, NX):
        low_sum = low_sum + arr_a[step - 1].astype(F32) * jnp.where(a >= step, 1.0, 0.0).astype(F32)
    for copy in phase_b:
        copy.wait_recv()
    for step in range(1, NX):
        low_sum = low_sum + arr_b[step - 1].astype(F32)
    back[...] = (low_sum + core0 * s_full[mine]).astype(BF16)
    last = remote(back, state.at[mine], p_send.at[1], p_recv.at[1], sibling)
    last.start()
    state[mine] = (low_sum + core1 * sib[...].astype(F32)).astype(BF16)

    others = pl.ds(1, NZ - 1)
    for copy in weight_z:
        copy.wait_recv()

    def share_rows(step):
        return pl.ds(pl.multiple_of(c * 256 + b * 64 + lax.rem(a + step, NX) * 16, 16), 16)

    def group_rows(step):
        return pl.ds(pl.multiple_of(c * 256 + lax.rem(b + step, NX) * 64, 64), 64)

    def ring_starts(rows, peer, send_sem, recv_sem):
        piece = weight.at[others, rows(0)]
        up = remote(piece, piece, send_sem.at[0], recv_sem.at[0], peer(1))
        down = remote(piece, piece, send_sem.at[1], recv_sem.at[1], peer(NX - 1))
        up.start()
        down.start()
        return [up, down]

    def ring_forwards(rows, peer, send_sem, recv_sem, copies):
        copies[0].wait_recv()
        from_below = weight.at[others, rows(NX - 1), pl.ds(0, HALF)]
        up = remote(from_below, from_below, send_sem.at[2], recv_sem.at[2], peer(1))
        up.start()
        copies[1].wait_recv()
        from_above = weight.at[others, rows(1), pl.ds(HALF, HALF)]
        down = remote(from_above, from_above, send_sem.at[3], recv_sem.at[3], peer(NX - 1))
        down.start()
        return [up, down]

    ring_a = ring_starts(share_rows, a_peer, wa_send, wa_recv)

    last.wait_recv()

    def slot_send(index, hop, chunk, up):
        rows = pl.ds(pl.multiple_of(chunk * CHUNK, CHUNK), CHUNK)
        if up:
            src, dst = lax.rem(NZ + 1 - hop, NZ), NZ - hop
            return remote(
                gathered.at[src, rows], gathered.at[dst, rows],
                r_send.at[index], r_recv.at[index], z_peer(1),
            )
        return remote(
            gathered.at[hop - 1, rows], gathered.at[hop, rows],
            l_send.at[index], l_recv.at[index], z_peer(NZ - 1),
        )

    ss_own[...] = jnp.zeros_like(ss_own)
    for chunk in range(NCHUNK):
        rows = slice(chunk * CHUNK, (chunk + 1) * CHUNK)
        squares = jnp.zeros((CHUNK, HEAD_DIM), F32)
        for h in range(4):
            att = within[rows, head(h)] + contract(aq[rows, head(h)], state[h], 1, 0)
            squares = squares + att * att
            gathered[0, rows, head(h)] = (att * gate[rows, head(h)]).astype(BF16)
        slot_send(chunk, 1, chunk, True).start()
        slot_send(chunk, 1, chunk, False).start()
        ss_own[chunk : chunk + 1, :] = jnp.sum(squares.T, axis=0, keepdims=True)

    square_sends = []
    for step in range(1, NZ):
        copy = remote(
            ss_own, ss_all.at[step - 1], ss_send.at[step - 1], ss_recv.at[step - 1], z_peer(step)
        )
        copy.start()
        square_sends.append(copy)

    def project(slot, row, count, fresh=False):
        rows = pl.ds(pl.multiple_of(row, CHUNK), count)
        for n in range(OUT // 256):
            cols = slice(n * 256, (n + 1) * 256)
            term = jnp.dot(
                gathered[slot, rows, :], weight[slot, :, cols], preferred_element_type=F32
            )
            if fresh:
                acc[rows, cols] = term
            else:
                acc[rows, cols] += term

    load_w.wait()
    for part in range(2):
        project(0, part * 256, 256, fresh=True)

    def pass_on(index, _):
        hop = lax.div(index, NCHUNK) + 1
        chunk = lax.rem(index, NCHUNK)
        slot_send(index, hop, chunk, True).wait_recv()
        slot_send(index + NCHUNK, hop + 1, chunk, True).start()
        slot_send(index, hop, chunk, False).wait_recv()
        slot_send(index + NCHUNK, hop + 1, chunk, False).start()
        return 0

    def pass_range(start, stop):
        lax.fori_loop(start, stop, pass_on, 0)

    pass_range(0, 1)
    ring_a2 = ring_forwards(share_rows, a_peer, wa_send, wa_recv, ring_a)
    pass_range(1, 2)
    for copy in ring_a2:
        copy.wait_recv()
    ring_b = ring_starts(group_rows, b_peer, wb_send, wb_recv)

    def to_sibling(step):
        piece = weight.at[others, group_rows(step)]
        copy = remote(piece, piece, ws_send.at[step], ws_recv.at[step], sibling)
        copy.start()
        return copy

    sibling_sends = [to_sibling(0)]
    pass_range(2, 5)
    ring_b2 = ring_forwards(group_rows, b_peer, wb_send, wb_recv, ring_b)
    sibling_sends.append(to_sibling(1))
    sibling_sends.append(to_sibling(3))
    pass_range(5, 7)
    for copy in ring_b2:
        copy.wait_recv()
    sibling_sends.append(to_sibling(2))
    pass_range(7, 8)
    for copy in sibling_sends:
        copy.wait_recv()

    def hop_three(chunk):
        index = 2 * NCHUNK + chunk
        slot_send(index, 3, chunk, True).wait_recv()
        if chunk < NCHUNK // 2:
            slot_send(index + NCHUNK, 4, chunk, True).start()
        slot_send(index, 3, chunk, False).wait_recv()
        if chunk >= NCHUNK // 2:
            slot_send(index + NCHUNK, 4, chunk, False).start()

    def project_whole(slot):
        def body(part, _):
            project(slot, part * 256, 256)
            return 0
        lax.fori_loop(0, 2, body, 0)

    hop_three(0)
    project_whole(7)
    hop_three(1)
    project_whole(1)
    hop_three(2)
    project_whole(6)
    hop_three(3)
    project_whole(2)
    project_whole(5)
    project_whole(3)

    for step in range(NZ - 1):
        square_sends[step].wait_recv()
    sums = ss_own[...]
    for step in range(NZ - 1):
        sums = sums + ss_all[step]
    factor = lax.rsqrt(sums / (HEADS * HEAD_DIM) + 1e-06)

    for pair in range(NCHUNK // 2):
        for chunk, up in ((pair, True), (pair + NCHUNK // 2, False)):
            slot_send(3 * NCHUNK + chunk, 4, chunk, up).wait_recv()
            project(4, chunk * CHUNK, CHUNK)
            rows = slice(chunk * CHUNK, (chunk + 1) * CHUNK)
            column = jnp.broadcast_to(factor[chunk : chunk + 1, :], (CHUNK, CHUNK)).T
            for n in range(OUT // 128):
                cols = slice(n * 128, (n + 1) * 128)
                out_ref[rows, cols] = (acc[rows, cols] * column).astype(BF16)

    first.wait_send()
    last.wait_send()
    for copy in (
        weight_z + phase_a + phase_b + square_sends
        + ring_a + ring_a2 + ring_b + ring_b2 + sibling_sends
    ):
        copy.wait_send()

    def drain(index, _):
        hop = lax.div(index, NCHUNK) + 1
        chunk = lax.rem(index, NCHUNK)
        slot_send(index, hop, chunk, True).wait_send()
        slot_send(index, hop, chunk, False).wait_send()
        return 0

    lax.fori_loop(0, 3 * NCHUNK, drain, 0)
    for chunk in range(NCHUNK):
        slot_send(3 * NCHUNK + chunk, 4, chunk, chunk < NCHUNK // 2).wait_send()


def body(queries, keys, values, gate_logits, out_weight):
    dma = pltpu.SemaphoreType.DMA
    pair = (2, HEAD_DIM, HEAD_DIM)
    vmem = pltpu.VMEM
    return pl.pallas_call(
        kernel,
        out_shape=jax.ShapeDtypeStruct((ROWS, OUT), BF16),
        in_specs=[pl.BlockSpec(memory_space=pl.ANY)] * 5,
        out_specs=pl.BlockSpec(memory_space=pltpu.VMEM),
        scratch_shapes=[
            vmem((ROWS, FEAT), BF16), vmem((ROWS, FEAT), BF16),
            vmem((ROWS, FEAT), BF16), vmem((ROWS, FEAT), BF16),
            vmem((ROWS, FEAT), BF16), vmem((ROWS, FEAT), BF16), vmem((ROWS, FEAT), BF16),
            vmem((ROWS, FEAT), F32), vmem((ROWS, FEAT), F32),
            vmem((4, HEAD_DIM, HEAD_DIM), F32), vmem((4, HEAD_DIM, HEAD_DIM), BF16),
            vmem(pair, BF16), vmem(pair, BF16), vmem((NX - 1,) + pair, BF16),
            vmem((2,) + pair, BF16), vmem((NX - 1,) + pair, BF16),
            vmem(pair, BF16), vmem((4, HEAD_DIM, HEAD_DIM), BF16),
            vmem((NZ, ROWS, FEAT), BF16), vmem((NZ, ROWS, OUT), BF16),
            vmem((ROWS, OUT), F32), vmem((8, 128), F32), vmem((NZ - 1, 8, 128), F32),
            dma((5,)), dma((NZ - 1,)), dma((NZ - 1,)), dma((2,)), dma((2,)),
            dma((NX - 1,)), dma((NX - 1,)), dma((NX - 1,)), dma((NX - 1,)),
            dma((NZ - 1,)), dma((NZ - 1,)),
            dma((4 * NCHUNK,)), dma((4 * NCHUNK,)), dma((4 * NCHUNK,)), dma((4 * NCHUNK,)),
            dma((4,)), dma((4,)), dma((4,)), dma((4,)), dma((4,)), dma((4,)),
        ],
        compiler_params=pltpu.CompilerParams(
            collective_id=0, has_side_effects=True, vmem_limit_bytes=48 * 1024 * 1024
        ),
        cost_estimate=pl.CostEstimate(
            flops=3_900_000_000, bytes_accessed=9_000_000, transcendentals=1_000_000
        ),
    )(queries, keys, values, gate_logits, out_weight)


def solution(mesh):
    return jax.shard_map(
        body,
        mesh=mesh,
        in_specs=(
            P("seq", "head"),
            P("seq", "head"),
            P("seq", "head"),
            P("seq", "head"),
            P("head", None),
        ),
        out_specs=P("seq", "head"),
        check_vma=False,
    )
```

```python
import functools

import jax
import jax.numpy as jnp
from jax import lax
from jax.experimental import pallas as pl
from jax.experimental.pallas import tpu as pltpu
from jax.sharding import PartitionSpec as P

HEADS = 32
HEAD_DIM = 128
F32 = jnp.float32
BF16 = jnp.bfloat16
MESH = pl.DeviceIdType.MESH

NX = 4
NZ = 8
ROWS = 512
FEAT = 512
OUT = 768
PAIR = 256
NCHUNK = 4
HALF = OUT // 2


def sigmoid(value):
    return 0.5 + 0.5 * jnp.tanh(0.5 * value)


def silu(raw):
    value = raw.astype(F32)
    return (value * sigmoid(value)).astype(BF16)


def contract(lhs, rhs, lhs_dim, rhs_dim):
    return lax.dot_general(
        lhs, rhs, (((lhs_dim,), (rhs_dim,)), ((), ())), preferred_element_type=F32
    )


def kernel(
    q_hbm, k_hbm, v_hbm, g_hbm, w_hbm, out_ref,
    q_in, k_in, v_in, g_in, aq, ak, av, within, gate, squares,
    s_full, s_bf, sib, tot_bf, low_sum, arr_a, pay, arr_b, back, state,
    gathered, weight, acc, ss_own, ss_all,
    load_sem, z_send, z_recv, p_send, p_recv, a_send, a_recv, b_send, b_recv,
    ss_send, ss_recv, r_send, r_recv, l_send, l_recv,
    wa_send, wa_recv, wb_send, wb_recv, ws_send, ws_recv,
):
    seq = lax.axis_index("seq")
    z = lax.axis_index("head")
    c = lax.rem(seq, 2)
    x = lax.rem(lax.div(seq, 2), NX)
    y = lax.div(seq, 2 * NX)
    a = x * (1 - c) + y * c
    b = y * (1 - c) + x * c

    def chip(x_step, y_step):
        x2 = lax.rem(x + x_step, NX)
        y2 = lax.rem(y + y_step, NX)
        return ((y2 * NX + x2) * 2 + c, z)

    def a_peer(step):
        return chip(step * (1 - c), step * c)

    def b_peer(step):
        return chip(step * c, step * (1 - c))

    def z_peer(step):
        return (seq, lax.rem(z + step, NZ))

    sibling = (seq + 1 - 2 * c, z)

    def remote(src, dst, send_sem, recv_sem, device):
        return pltpu.make_async_remote_copy(
            src_ref=src, dst_ref=dst, send_sem=send_sem, recv_sem=recv_sem,
            device_id=device, device_id_type=MESH,
        )

    barrier = pltpu.get_barrier_semaphore()
    partners = (
        [sibling]
        + [chip(step, 0) for step in range(1, NX)]
        + [chip(0, step) for step in range(1, NX)]
        + [z_peer(step) for step in range(1, NZ)]
    )
    for partner in partners:
        pl.semaphore_signal(barrier, inc=1, device_id=partner, device_id_type=MESH)

    def load(src, dst, index):
        copy = pltpu.make_async_copy(src, dst, load_sem.at[index])
        copy.start()
        return copy

    def head(h):
        return slice(h * HEAD_DIM, (h + 1) * HEAD_DIM)

    loads_kv = []
    for stage in range(2):
        part = pl.ds(stage * PAIR, PAIR)
        loads_kv.append((
            load(k_hbm.at[:, part], k_in.at[:, part], 2 * stage),
            load(v_hbm.at[:, part], v_in.at[:, part], 2 * stage + 1),
        ))
    load_q = load(q_hbm, q_in, 4)
    load_g = load(g_hbm, g_in, 5)
    own_columns = pl.ds(pl.multiple_of(z * OUT, 128), OUT)
    load_w = load(w_hbm.at[:, own_columns], weight.at[0], 6)

    def stage_heads(stage):
        return pl.ds(2 * stage, 2)

    def to_core1(stage):
        return remote(
            s_bf.at[stage_heads(stage)], sib.at[stage_heads(stage)],
            p_send.at[stage], p_recv.at[stage], sibling,
        )

    def to_core0(stage):
        return remote(
            back.at[stage_heads(stage)], state.at[stage_heads(stage)],
            p_send.at[2 + stage], p_recv.at[2 + stage], sibling,
        )

    def first_phase(h, step):
        index = h * (NX - 1) + step - 1
        device = chip(step, 0) if h % 2 == 0 else chip(0, step)
        return remote(
            tot_bf.at[h], arr_a.at[h, step - 1], a_send.at[index], a_recv.at[index], device
        )

    def second_phase(h, step):
        index = h * (NX - 1) + step - 1
        device = chip(0, step) if h % 2 == 0 else chip(step, 0)
        place = y if h % 2 == 0 else x
        return remote(
            pay.at[h, lax.div(place + step, NX)], arr_b.at[h, step - 1],
            b_send.at[index], b_recv.at[index], device,
        )

    def local_states(stage):
        for copy in loads_kv[stage]:
            copy.wait()
        for h in (2 * stage, 2 * stage + 1):
            ak[:, head(h)] = silu(k_in[:, head(h)])
            av[:, head(h)] = silu(v_in[:, head(h)])
            outer = contract(ak[:, head(h)], av[:, head(h)], 0, 0)
            s_full[h] = outer
            s_bf[h] = outer.astype(BF16)

    local_states(0)
    pl.semaphore_wait(barrier, len(partners))
    pl.when(c == 0)(lambda: to_core1(0).start())
    local_states(1)
    pl.when(c == 0)(lambda: to_core1(1).start())

    @pl.when(c == 1)
    def _():
        for stage in range(2):
            to_core1(stage).wait_recv()
            for h in (2 * stage, 2 * stage + 1):
                tot_bf[h] = (s_full[h] + sib[h].astype(F32)).astype(BF16)
                for step in range(1, NX):
                    first_phase(h, step).start()

    share = pl.multiple_of(c * 256 + b * 64 + a * 16, 16)
    weight_z = []
    for step in range(1, NZ):
        columns = pl.ds(pl.multiple_of(lax.rem(z + step, NZ) * OUT, 128), OUT)
        copy = remote(
            w_hbm.at[pl.ds(share, 16), columns],
            weight.at[NZ - step, pl.ds(share, 16)],
            z_send.at[step - 1], z_recv.at[step - 1], z_peer(step),
        )
        copy.start()
        weight_z.append(copy)

    half = ROWS // 2
    row_id = lax.broadcasted_iota(jnp.int32, (half, half), 0)
    col_id = lax.broadcasted_iota(jnp.int32, (half, half), 1)
    causal = row_id >= col_id

    def attend_block(h):
        for part in range(2):
            rows = slice(part * half, (part + 1) * half)
            qh = aq[rows, head(h)]
            diag = contract(qh, ak[rows, head(h)], 1, 1)
            diag = jnp.where(causal, diag, 0.0).astype(BF16)
            result = contract(diag, av[rows, head(h)], 1, 0)
            if part == 1:
                low = contract(qh, ak[0:half, head(h)], 1, 1).astype(BF16)
                result = result + contract(low, av[0:half, head(h)], 1, 0)
            within[rows, head(h)] = result

    load_q.wait()
    for h in range(4):
        aq[:, head(h)] = silu(q_in[:, head(h)])
    attend_block(0)
    attend_block(1)

    def turn(stage):
        for h in (2 * stage, 2 * stage + 1):
            place = x if h % 2 == 0 else y
            total = s_full[h] + sib[h].astype(F32)
            lower = jnp.zeros((HEAD_DIM, HEAD_DIM), F32)
            whole = total
            for step in range(1, NX):
                first_phase(h, step).wait_recv()
                term = arr_a[h, step - 1].astype(F32)
                lower = lower + term * jnp.where(place >= step, 1.0, 0.0).astype(F32)
                whole = whole + term
            low_sum[h] = lower
            if h % 2 == 0:
                pay[h, 0] = whole.astype(BF16)
                pay[h, 1] = jnp.zeros((HEAD_DIM, HEAD_DIM), BF16)
            else:
                pay[h, 0] = (lower + total).astype(BF16)
                pay[h, 1] = lower.astype(BF16)
            for step in range(1, NX):
                second_phase(h, step).start()

    pl.when(c == 1)(lambda: turn(0))
    attend_block(2)
    pl.when(c == 1)(lambda: turn(1))
    attend_block(3)
    load_g.wait()
    for h in range(4):
        gate[:, head(h)] = sigmoid(g_in[:, head(h)].astype(F32))

    def finish_state(stage):
        @pl.when(c == 1)
        def _():
            for h in (2 * stage, 2 * stage + 1):
                before = low_sum[h]
                for step in range(1, NX):
                    second_phase(h, step).wait_recv()
                    before = before + arr_b[h, step - 1].astype(F32)
                back[h] = before.astype(BF16)
                state[h] = (before + sib[h].astype(F32)).astype(BF16)
            to_core0(stage).start()

        @pl.when(c == 0)
        def _():
            to_core0(stage).wait_recv()

    def slot_send(index, hop, chunk, up):
        part = lax.div(chunk, 2)
        rows = pl.ds(pl.multiple_of(lax.rem(chunk, 2) * half, half), half)
        if up:
            src, dst = lax.rem(NZ + 1 - hop, NZ), NZ - hop
            return remote(
                gathered.at[src, part, rows], gathered.at[dst, part, rows],
                r_send.at[index], r_recv.at[index], z_peer(1),
            )
        return remote(
            gathered.at[hop - 1, part, rows], gathered.at[hop, part, rows],
            l_send.at[index], l_recv.at[index], z_peer(NZ - 1),
        )

    def finish_attended(stage):
        for part in range(2):
            rows = slice(part * half, (part + 1) * half)
            total = jnp.zeros((half, HEAD_DIM), F32) if stage == 0 else squares[rows, :]
            for i in range(2):
                h = 2 * stage + i
                att = within[rows, head(h)] + contract(aq[rows, head(h)], state[h], 1, 0)
                total = total + att * att
                gathered[0, stage, rows, head(i)] = (att * gate[rows, head(h)]).astype(BF16)
            squares[rows, :] = total
            chunk = 2 * stage + part
            slot_send(chunk, 1, chunk, True).start()
            slot_send(chunk, 1, chunk, False).start()

    finish_state(0)
    finish_attended(0)
    finish_state(1)
    finish_attended(1)
    ss_own[...] = jnp.zeros_like(ss_own)
    for group in range(ROWS // 128):
        tile = squares[group * 128 : (group + 1) * 128, :]
        ss_own[group : group + 1, :] = jnp.sum(tile.T, axis=0, keepdims=True)

    square_sends = []
    for step in range(1, NZ):
        copy = remote(
            ss_own, ss_all.at[step - 1], ss_send.at[step - 1], ss_recv.at[step - 1], z_peer(step)
        )
        copy.start()
        square_sends.append(copy)

    others = pl.ds(1, NZ - 1)
    for copy in weight_z:
        copy.wait_recv()

    def share_rows(step):
        return pl.ds(pl.multiple_of(c * 256 + b * 64 + lax.rem(a + step, NX) * 16, 16), 16)

    def group_rows(step):
        return pl.ds(pl.multiple_of(c * 256 + lax.rem(b + step, NX) * 64, 64), 64)

    def ring_starts(rows, peer, send_sem, recv_sem):
        piece = weight.at[others, rows(0)]
        up = remote(piece, piece, send_sem.at[0], recv_sem.at[0], peer(1))
        down = remote(piece, piece, send_sem.at[1], recv_sem.at[1], peer(NX - 1))
        up.start()
        down.start()
        return [up, down]

    def ring_forwards(rows, peer, send_sem, recv_sem, copies):
        copies[0].wait_recv()
        from_below = weight.at[others, rows(NX - 1), pl.ds(0, HALF)]
        up = remote(from_below, from_below, send_sem.at[2], recv_sem.at[2], peer(1))
        up.start()
        copies[1].wait_recv()
        from_above = weight.at[others, rows(1), pl.ds(HALF, HALF)]
        down = remote(from_above, from_above, send_sem.at[3], recv_sem.at[3], peer(NX - 1))
        down.start()
        return [up, down]

    ring_a = ring_starts(share_rows, a_peer, wa_send, wa_recv)

    def project(slot, row, count, fresh=False):
        rows = pl.ds(pl.multiple_of(row, 128), count)
        for n in range(OUT // 256):
            cols = slice(n * 256, (n + 1) * 256)
            term = contract(gathered[slot, 0, rows, :], weight[slot, 0:PAIR, cols], 1, 0)
            term = term + contract(gathered[slot, 1, rows, :], weight[slot, PAIR:FEAT, cols], 1, 0)
            if fresh:
                acc[rows, cols] = term
            else:
                acc[rows, cols] += term

    load_w.wait()
    for part in range(2):
        project(0, part * 256, 256, fresh=True)

    def pass_on(index, _):
        hop = lax.div(index, NCHUNK) + 1
        chunk = lax.rem(index, NCHUNK)
        slot_send(index, hop, chunk, True).wait_recv()
        slot_send(index + NCHUNK, hop + 1, chunk, True).start()
        slot_send(index, hop, chunk, False).wait_recv()
        slot_send(index + NCHUNK, hop + 1, chunk, False).start()
        return 0

    def pass_range(start, stop):
        lax.fori_loop(start, stop, pass_on, 0)

    pass_range(0, 1)
    ring_a2 = ring_forwards(share_rows, a_peer, wa_send, wa_recv, ring_a)
    pass_range(1, 2)
    for copy in ring_a2:
        copy.wait_recv()
    ring_b = ring_starts(group_rows, b_peer, wb_send, wb_recv)

    def to_sibling(step):
        piece = weight.at[others, group_rows(step)]
        copy = remote(piece, piece, ws_send.at[step], ws_recv.at[step], sibling)
        copy.start()
        return copy

    sibling_sends = [to_sibling(0)]
    pass_range(2, 5)
    ring_b2 = ring_forwards(group_rows, b_peer, wb_send, wb_recv, ring_b)
    sibling_sends.append(to_sibling(1))
    sibling_sends.append(to_sibling(3))
    pass_range(5, 7)
    for copy in ring_b2:
        copy.wait_recv()
    sibling_sends.append(to_sibling(2))
    pass_range(7, 8)
    for copy in sibling_sends:
        copy.wait_recv()

    def hop_three(chunk):
        index = 2 * NCHUNK + chunk
        slot_send(index, 3, chunk, True).wait_recv()
        if chunk < NCHUNK // 2:
            slot_send(index + NCHUNK, 4, chunk, True).start()
        slot_send(index, 3, chunk, False).wait_recv()
        if chunk >= NCHUNK // 2:
            slot_send(index + NCHUNK, 4, chunk, False).start()

    def project_whole(slot):
        def body(part, _):
            project(slot, part * 256, 256)
            return 0
        lax.fori_loop(0, 2, body, 0)

    hop_three(0)
    project_whole(7)
    hop_three(1)
    project_whole(1)
    hop_three(2)
    project_whole(6)
    hop_three(3)
    project_whole(2)
    project_whole(5)
    project_whole(3)

    for step in range(NZ - 1):
        square_sends[step].wait_recv()
    sums = ss_own[...]
    for step in range(NZ - 1):
        sums = sums + ss_all[step]
    factor = lax.rsqrt(sums / (HEADS * HEAD_DIM) + 1e-06)

    for part in range(2):
        slot_send(3 * NCHUNK + part, 4, part, True).wait_recv()
        slot_send(3 * NCHUNK + part + 2, 4, part + 2, False).wait_recv()
        project(4, part * half, half)
        for group in (2 * part, 2 * part + 1):
            rows = slice(group * 128, (group + 1) * 128)
            column = jnp.broadcast_to(factor[group : group + 1, :], (128, 128)).T
            for n in range(OUT // 128):
                cols = slice(n * 128, (n + 1) * 128)
                out_ref[rows, cols] = (acc[rows, cols] * column).astype(BF16)

    @pl.when(c == 0)
    def _():
        for stage in range(2):
            to_core1(stage).wait_send()

    @pl.when(c == 1)
    def _():
        for stage in range(2):
            to_core0(stage).wait_send()
        for h in range(4):
            for step in range(1, NX):
                first_phase(h, step).wait_send()
                second_phase(h, step).wait_send()

    for copy in (
        weight_z + square_sends + ring_a + ring_a2 + ring_b + ring_b2 + sibling_sends
    ):
        copy.wait_send()

    def drain(index, _):
        hop = lax.div(index, NCHUNK) + 1
        chunk = lax.rem(index, NCHUNK)
        slot_send(index, hop, chunk, True).wait_send()
        slot_send(index, hop, chunk, False).wait_send()
        return 0

    lax.fori_loop(0, 3 * NCHUNK, drain, 0)
    for chunk in range(NCHUNK):
        slot_send(3 * NCHUNK + chunk, 4, chunk, chunk < NCHUNK // 2).wait_send()


def body(*arrays):
    dma = pltpu.SemaphoreType.DMA
    full = (4, HEAD_DIM, HEAD_DIM)
    vmem = pltpu.VMEM
    return pl.pallas_call(
        kernel,
        out_shape=jax.ShapeDtypeStruct((ROWS, OUT), BF16),
        in_specs=[pl.BlockSpec(memory_space=pl.ANY)] * 5,
        out_specs=pl.BlockSpec(memory_space=pltpu.VMEM),
        scratch_shapes=[
            vmem((ROWS, FEAT), BF16), vmem((ROWS, FEAT), BF16),
            vmem((ROWS, FEAT), BF16), vmem((ROWS, FEAT), BF16),
            vmem((ROWS, FEAT), BF16), vmem((ROWS, FEAT), BF16), vmem((ROWS, FEAT), BF16),
            vmem((ROWS, FEAT), F32), vmem((ROWS, FEAT), F32), vmem((ROWS, HEAD_DIM), F32),
            vmem(full, F32), vmem(full, BF16), vmem(full, BF16), vmem(full, BF16), vmem(full, F32),
            vmem((4, NX - 1, HEAD_DIM, HEAD_DIM), BF16), vmem((4, 2, HEAD_DIM, HEAD_DIM), BF16),
            vmem((4, NX - 1, HEAD_DIM, HEAD_DIM), BF16), vmem(full, BF16), vmem(full, BF16),
            vmem((NZ, 2, ROWS, PAIR), BF16), vmem((NZ, ROWS, OUT), BF16),
            vmem((ROWS, OUT), F32), vmem((8, 128), F32), vmem((NZ - 1, 8, 128), F32),
            dma((7,)), dma((NZ - 1,)), dma((NZ - 1,)), dma((4,)), dma((4,)),
            dma((12,)), dma((12,)), dma((12,)), dma((12,)),
            dma((NZ - 1,)), dma((NZ - 1,)),
            dma((4 * NCHUNK,)), dma((4 * NCHUNK,)), dma((4 * NCHUNK,)), dma((4 * NCHUNK,)),
            dma((4,)), dma((4,)), dma((4,)), dma((4,)), dma((4,)), dma((4,)),
        ],
        compiler_params=pltpu.CompilerParams(
            collective_id=0, has_side_effects=True, vmem_limit_bytes=48 * 1024 * 1024
        ),
        cost_estimate=pl.CostEstimate(
            flops=3_900_000_000, bytes_accessed=9_000_000, transcendentals=1_000_000
        ),
    )(*(pltpu.with_memory_space_constraint(arg, pltpu.HBM) for arg in arrays))


def solution(mesh):
    return jax.shard_map(
        body,
        mesh=mesh,
        in_specs=(
            P("seq", "head"),
            P("seq", "head"),
            P("seq", "head"),
            P("seq", "head"),
            P("head", None),
        ),
        out_specs=P("seq", "head"),
        check_vma=False,
    )
```

```python
import functools

import jax
import jax.numpy as jnp
from jax import lax
from jax.experimental import pallas as pl
from jax.experimental.pallas import tpu as pltpu
from jax.sharding import PartitionSpec as P

HEADS = 32
HEAD_DIM = 128
F32 = jnp.float32
BF16 = jnp.bfloat16
MESH = pl.DeviceIdType.MESH

NX = 4
NZ = 8
STEPS = (2, 1, 3)
ROWS = 512
FEAT = 512
OUT = 768
PAIR = 256
NCHUNK = 4
HALF = OUT // 2


def sigmoid(value):
    return 0.5 + 0.5 * jnp.tanh(0.5 * value)


def silu(raw):
    value = raw.astype(F32)
    return (value * sigmoid(value)).astype(BF16)


def contract(lhs, rhs, lhs_dim, rhs_dim):
    return lax.dot_general(
        lhs, rhs, (((lhs_dim,), (rhs_dim,)), ((), ())), preferred_element_type=F32
    )


def kernel(
    q_hbm, k_hbm, v_hbm, g_hbm, w_hbm, out_ref,
    q_in, k_in, v_in, g_in, aq, ak, av, within, gate, squares,
    s_full, s_bf, sib, tot_bf, low_sum, arr_a, pay, arr_b, back, state,
    gathered, weight, acc, ss_own, ss_all,
    near, load_sem, z_send, z_recv, p_send, p_recv, a_send, a_recv, b_send, b_recv,
    ss_send, ss_recv, r_send, r_recv, l_send, l_recv,
    wa_send, wa_recv, wb_send, wb_recv, ws_send, ws_recv,
):
    seq = lax.axis_index("seq")
    z = lax.axis_index("head")
    c = lax.rem(seq, 2)
    x = lax.rem(lax.div(seq, 2), NX)
    y = lax.div(seq, 2 * NX)
    a = x * (1 - c) + y * c
    b = y * (1 - c) + x * c

    def chip(x_step, y_step):
        x2 = lax.rem(x + x_step, NX)
        y2 = lax.rem(y + y_step, NX)
        return ((y2 * NX + x2) * 2 + c, z)

    def a_peer(step):
        return chip(step * (1 - c), step * c)

    def b_peer(step):
        return chip(step * c, step * (1 - c))

    def z_peer(step):
        return (seq, lax.rem(z + step, NZ))

    sibling = (seq + 1 - 2 * c, z)

    def remote(src, dst, send_sem, recv_sem, device):
        return pltpu.make_async_remote_copy(
            src_ref=src, dst_ref=dst, send_sem=send_sem, recv_sem=recv_sem,
            device_id=device, device_id_type=MESH,
        )

    barrier = pltpu.get_barrier_semaphore()
    partners = (
        [sibling]
        + [chip(step, 0) for step in range(1, NX)]
        + [chip(0, step) for step in range(1, NX)]
        + [z_peer(1), z_peer(NZ - 1)]
    )
    for partner in partners:
        pl.semaphore_signal(barrier, inc=1, device_id=partner, device_id_type=MESH)

    def load(src, dst, index):
        copy = pltpu.make_async_copy(src, dst, load_sem.at[index])
        copy.start()
        return copy

    def head(h):
        return slice(h * HEAD_DIM, (h + 1) * HEAD_DIM)

    loads_kv = []
    for stage in range(2):
        part = pl.ds(stage * PAIR, PAIR)
        loads_kv.append((
            load(k_hbm.at[:, part], k_in.at[:, part], 2 * stage),
            load(v_hbm.at[:, part], v_in.at[:, part], 2 * stage + 1),
        ))
    load_q = load(q_hbm, q_in, 4)
    load_g = load(g_hbm, g_in, 5)
    own_columns = pl.ds(pl.multiple_of(z * OUT, 128), OUT)
    load_w = load(w_hbm.at[:, own_columns], weight.at[0], 6)

    def stage_heads(stage):
        return pl.ds(2 * stage, 2)

    def to_core1(stage):
        return remote(
            s_bf.at[stage_heads(stage)], sib.at[stage_heads(stage)],
            p_send.at[stage], p_recv.at[stage], sibling,
        )

    def to_core0(stage):
        return remote(
            back.at[stage_heads(stage)], state.at[stage_heads(stage)],
            p_send.at[2 + stage], p_recv.at[2 + stage], sibling,
        )

    def first_phase(h, step):
        index = h * (NX - 1) + step - 1
        device = chip(step, 0) if h % 2 == 0 else chip(0, step)
        return remote(
            tot_bf.at[h], arr_a.at[h, step - 1], a_send.at[index], a_recv.at[index], device
        )

    def second_phase(h, step):
        index = h * (NX - 1) + step - 1
        device = chip(0, step) if h % 2 == 0 else chip(step, 0)
        place = y if h % 2 == 0 else x
        return remote(
            pay.at[h, lax.div(place + step, NX)], arr_b.at[h, step - 1],
            b_send.at[index], b_recv.at[index], device,
        )

    def local_state(h):
        ak[:, head(h)] = silu(k_in[:, head(h)])
        av[:, head(h)] = silu(v_in[:, head(h)])
        outer = contract(ak[:, head(h)], av[:, head(h)], 0, 0)
        s_full[h] = outer
        s_bf[h] = outer.astype(BF16)

    def depart(stage):
        to_core1(stage).wait_recv()
        for h in (2 * stage, 2 * stage + 1):
            tot_bf[h] = (s_full[h] + sib[h].astype(F32)).astype(BF16)
            for step in STEPS:
                first_phase(h, step).start()

    def greet(index, distance):
        for step in (distance, NZ - distance):
            pl.semaphore_signal(
                near.at[index], inc=1, device_id=z_peer(step), device_id_type=MESH
            )

    for copy in loads_kv[0]:
        copy.wait()
    local_state(0)
    local_state(1)
    pl.semaphore_wait(barrier, len(partners))
    pl.when(c == 0)(lambda: to_core1(0).start())
    greet(0, 1)
    for copy in loads_kv[1]:
        copy.wait()
    local_state(2)
    pl.when(c == 1)(lambda: depart(0))
    pl.semaphore_wait(near.at[0], 2)
    greet(1, 2)
    local_state(3)
    pl.when(c == 0)(lambda: to_core1(1).start())
    pl.when(c == 1)(lambda: depart(1))

    share = pl.multiple_of(c * 256 + b * 64 + a * 16, 16)
    pl.semaphore_wait(near.at[1], 2)
    weight_z = []
    for step in range(1, NZ):
        columns = pl.ds(pl.multiple_of(lax.rem(z + step, NZ) * OUT, 128), OUT)
        copy = remote(
            w_hbm.at[pl.ds(share, 16), columns],
            weight.at[NZ - step, pl.ds(share, 16)],
            z_send.at[step - 1], z_recv.at[step - 1], z_peer(step),
        )
        copy.start()
        weight_z.append(copy)

    half = ROWS // 2
    row_id = lax.broadcasted_iota(jnp.int32, (half, half), 0)
    col_id = lax.broadcasted_iota(jnp.int32, (half, half), 1)
    causal = row_id >= col_id

    def attend_block(h):
        for part in range(2):
            rows = slice(part * half, (part + 1) * half)
            qh = aq[rows, head(h)]
            diag = contract(qh, ak[rows, head(h)], 1, 1)
            diag = jnp.where(causal, diag, 0.0).astype(BF16)
            result = contract(diag, av[rows, head(h)], 1, 0)
            if part == 1:
                low = contract(qh, ak[0:half, head(h)], 1, 1).astype(BF16)
                result = result + contract(low, av[0:half, head(h)], 1, 0)
            within[rows, head(h)] = result

    load_q.wait()
    for h in range(4):
        aq[:, head(h)] = silu(q_in[:, head(h)])
    attend_block(0)
    attend_block(1)

    def turn(stage):
        for h in (2 * stage, 2 * stage + 1):
            place = x if h % 2 == 0 else y
            total = s_full[h] + sib[h].astype(F32)
            lower = jnp.zeros((HEAD_DIM, HEAD_DIM), F32)
            whole = total
            for step in range(1, NX):
                first_phase(h, step).wait_recv()
                term = arr_a[h, step - 1].astype(F32)
                lower = lower + term * jnp.where(place >= step, 1.0, 0.0).astype(F32)
                whole = whole + term
            low_sum[h] = lower
            if h % 2 == 0:
                pay[h, 0] = whole.astype(BF16)
                pay[h, 1] = jnp.zeros((HEAD_DIM, HEAD_DIM), BF16)
            else:
                pay[h, 0] = (lower + total).astype(BF16)
                pay[h, 1] = lower.astype(BF16)
            for step in STEPS:
                second_phase(h, step).start()

    pl.when(c == 1)(lambda: turn(0))
    attend_block(2)
    pl.when(c == 1)(lambda: turn(1))
    attend_block(3)
    load_g.wait()
    for h in range(4):
        gate[:, head(h)] = sigmoid(g_in[:, head(h)].astype(F32))

    def finish_state(stage):
        @pl.when(c == 1)
        def _():
            for h in (2 * stage, 2 * stage + 1):
                before = low_sum[h]
                for step in range(1, NX):
                    second_phase(h, step).wait_recv()
                    before = before + arr_b[h, step - 1].astype(F32)
                back[h] = before.astype(BF16)
                state[h] = (before + sib[h].astype(F32)).astype(BF16)
            to_core0(stage).start()

        @pl.when(c == 0)
        def _():
            to_core0(stage).wait_recv()

    def slot_send(index, hop, chunk, up):
        part = lax.div(chunk, 2)
        rows = pl.ds(pl.multiple_of(lax.rem(chunk, 2) * half, half), half)
        if up:
            src, dst = lax.rem(NZ + 1 - hop, NZ), NZ - hop
            return remote(
                gathered.at[src, part, rows], gathered.at[dst, part, rows],
                r_send.at[index], r_recv.at[index], z_peer(1),
            )
        return remote(
            gathered.at[hop - 1, part, rows], gathered.at[hop, part, rows],
            l_send.at[index], l_recv.at[index], z_peer(NZ - 1),
        )

    def finish_attended(stage):
        for part in range(2):
            rows = slice(part * half, (part + 1) * half)
            total = jnp.zeros((half, HEAD_DIM), F32) if stage == 0 else squares[rows, :]
            for i in range(2):
                h = 2 * stage + i
                att = within[rows, head(h)] + contract(aq[rows, head(h)], state[h], 1, 0)
                total = total + att * att
                gathered[0, stage, rows, head(i)] = (att * gate[rows, head(h)]).astype(BF16)
            squares[rows, :] = total
            chunk = 2 * stage + part
            slot_send(chunk, 1, chunk, True).start()
            slot_send(chunk, 1, chunk, False).start()

    finish_state(0)
    finish_attended(0)
    finish_state(1)
    finish_attended(1)
    ss_own[...] = jnp.zeros_like(ss_own)
    for group in range(ROWS // 128):
        tile = squares[group * 128 : (group + 1) * 128, :]
        ss_own[group : group + 1, :] = jnp.sum(tile.T, axis=0, keepdims=True)

    square_sends = []
    for step in range(1, NZ):
        copy = remote(
            ss_own, ss_all.at[step - 1], ss_send.at[step - 1], ss_recv.at[step - 1], z_peer(step)
        )
        copy.start()
        square_sends.append(copy)

    others = pl.ds(1, NZ - 1)

    def share_rows(step):
        return pl.ds(pl.multiple_of(c * 256 + b * 64 + lax.rem(a + step, NX) * 16, 16), 16)

    def group_rows(step):
        return pl.ds(pl.multiple_of(c * 256 + lax.rem(b + step, NX) * 64, 64), 64)

    def ring_starts(rows, peer, send_sem, recv_sem):
        piece = weight.at[others, rows(0)]
        up = remote(piece, piece, send_sem.at[0], recv_sem.at[0], peer(1))
        down = remote(piece, piece, send_sem.at[1], recv_sem.at[1], peer(NX - 1))
        up.start()
        down.start()
        return [up, down]

    def ring_forwards(rows, peer, send_sem, recv_sem, copies):
        copies[0].wait_recv()
        from_below = weight.at[others, rows(NX - 1), pl.ds(0, HALF)]
        up = remote(from_below, from_below, send_sem.at[2], recv_sem.at[2], peer(1))
        up.start()
        copies[1].wait_recv()
        from_above = weight.at[others, rows(1), pl.ds(HALF, HALF)]
        down = remote(from_above, from_above, send_sem.at[3], recv_sem.at[3], peer(NX - 1))
        down.start()
        return [up, down]


    def project(slot, row, count, fresh=False):
        rows = pl.ds(pl.multiple_of(row, 128), count)
        for n in range(OUT // 256):
            cols = slice(n * 256, (n + 1) * 256)
            term = contract(gathered[slot, 0, rows, :], weight[slot, 0:PAIR, cols], 1, 0)
            term = term + contract(gathered[slot, 1, rows, :], weight[slot, PAIR:FEAT, cols], 1, 0)
            if fresh:
                acc[rows, cols] = term
            else:
                acc[rows, cols] += term

    load_w.wait()
    for part in range(2):
        project(0, part * 256, 256, fresh=True)

    def pass_on(index, _):
        hop = lax.div(index, NCHUNK) + 1
        chunk = lax.rem(index, NCHUNK)
        slot_send(index, hop, chunk, True).wait_recv()
        slot_send(index + NCHUNK, hop + 1, chunk, True).start()
        slot_send(index, hop, chunk, False).wait_recv()
        slot_send(index + NCHUNK, hop + 1, chunk, False).start()
        return 0

    def pass_range(start, stop):
        lax.fori_loop(start, stop, pass_on, 0)

    for copy in weight_z:
        copy.wait_recv()
    ring_a = ring_starts(share_rows, a_peer, wa_send, wa_recv)
    pass_range(0, 1)
    ring_a2 = ring_forwards(share_rows, a_peer, wa_send, wa_recv, ring_a)
    pass_range(1, 2)
    for copy in ring_a2:
        copy.wait_recv()
    ring_b = ring_starts(group_rows, b_peer, wb_send, wb_recv)

    def to_sibling(step):
        piece = weight.at[others, group_rows(step)]
        copy = remote(piece, piece, ws_send.at[step], ws_recv.at[step], sibling)
        copy.start()
        return copy

    sibling_sends = [to_sibling(0)]
    pass_range(2, 5)
    ring_b2 = ring_forwards(group_rows, b_peer, wb_send, wb_recv, ring_b)
    sibling_sends.append(to_sibling(1))
    sibling_sends.append(to_sibling(3))
    pass_range(5, 8)
    for copy in ring_b2:
        copy.wait_recv()
    sibling_sends.append(to_sibling(2))
    for copy in sibling_sends:
        copy.wait_recv()

    def hop_three(chunk):
        index = 2 * NCHUNK + chunk
        slot_send(index, 3, chunk, True).wait_recv()
        if chunk < NCHUNK // 2:
            slot_send(index + NCHUNK, 4, chunk, True).start()
        slot_send(index, 3, chunk, False).wait_recv()
        if chunk >= NCHUNK // 2:
            slot_send(index + NCHUNK, 4, chunk, False).start()

    def project_whole(slot):
        def body(part, _):
            project(slot, part * 256, 256)
            return 0
        lax.fori_loop(0, 2, body, 0)

    hop_three(0)
    project_whole(7)
    hop_three(1)
    project_whole(1)
    hop_three(2)
    project_whole(6)
    hop_three(3)
    project_whole(2)
    project_whole(5)
    project_whole(3)

    for step in range(NZ - 1):
        square_sends[step].wait_recv()
    sums = ss_own[...]
    for step in range(NZ - 1):
        sums = sums + ss_all[step]
    factor = lax.rsqrt(sums / (HEADS * HEAD_DIM) + 1e-06)

    for part in range(2):
        slot_send(3 * NCHUNK + part, 4, part, True).wait_recv()
        slot_send(3 * NCHUNK + part + 2, 4, part + 2, False).wait_recv()
        project(4, part * half, half)
        for group in (2 * part, 2 * part + 1):
            rows = slice(group * 128, (group + 1) * 128)
            column = jnp.broadcast_to(factor[group : group + 1, :], (128, 128)).T
            for n in range(OUT // 128):
                cols = slice(n * 128, (n + 1) * 128)
                out_ref[rows, cols] = (acc[rows, cols] * column).astype(BF16)

    @pl.when(c == 0)
    def _():
        for stage in range(2):
            to_core1(stage).wait_send()

    @pl.when(c == 1)
    def _():
        for stage in range(2):
            to_core0(stage).wait_send()
        for h in range(4):
            for step in range(1, NX):
                first_phase(h, step).wait_send()
                second_phase(h, step).wait_send()

    for copy in (
        weight_z + square_sends + ring_a + ring_a2 + ring_b + ring_b2 + sibling_sends
    ):
        copy.wait_send()

    def drain(index, _):
        hop = lax.div(index, NCHUNK) + 1
        chunk = lax.rem(index, NCHUNK)
        slot_send(index, hop, chunk, True).wait_send()
        slot_send(index, hop, chunk, False).wait_send()
        return 0

    lax.fori_loop(0, 3 * NCHUNK, drain, 0)
    for chunk in range(NCHUNK):
        slot_send(3 * NCHUNK + chunk, 4, chunk, chunk < NCHUNK // 2).wait_send()


def body(*arrays):
    dma = pltpu.SemaphoreType.DMA
    full = (4, HEAD_DIM, HEAD_DIM)
    vmem = pltpu.VMEM
    return pl.pallas_call(
        kernel,
        out_shape=jax.ShapeDtypeStruct((ROWS, OUT), BF16),
        in_specs=[pl.BlockSpec(memory_space=pl.ANY)] * 5,
        out_specs=pl.BlockSpec(memory_space=pltpu.VMEM),
        scratch_shapes=[
            vmem((ROWS, FEAT), BF16), vmem((ROWS, FEAT), BF16),
            vmem((ROWS, FEAT), BF16), vmem((ROWS, FEAT), BF16),
            vmem((ROWS, FEAT), BF16), vmem((ROWS, FEAT), BF16), vmem((ROWS, FEAT), BF16),
            vmem((ROWS, FEAT), F32), vmem((ROWS, FEAT), F32), vmem((ROWS, HEAD_DIM), F32),
            vmem(full, F32), vmem(full, BF16), vmem(full, BF16), vmem(full, BF16), vmem(full, F32),
            vmem((4, NX - 1, HEAD_DIM, HEAD_DIM), BF16), vmem((4, 2, HEAD_DIM, HEAD_DIM), BF16),
            vmem((4, NX - 1, HEAD_DIM, HEAD_DIM), BF16), vmem(full, BF16), vmem(full, BF16),
            vmem((NZ, 2, ROWS, PAIR), BF16), vmem((NZ, ROWS, OUT), BF16),
            vmem((ROWS, OUT), F32), vmem((8, 128), F32), vmem((NZ - 1, 8, 128), F32),
            pltpu.SemaphoreType.REGULAR((2,)), dma((7,)), dma((NZ - 1,)), dma((NZ - 1,)), dma((4,)), dma((4,)),
            dma((12,)), dma((12,)), dma((12,)), dma((12,)),
            dma((NZ - 1,)), dma((NZ - 1,)),
            dma((4 * NCHUNK,)), dma((4 * NCHUNK,)), dma((4 * NCHUNK,)), dma((4 * NCHUNK,)),
            dma((4,)), dma((4,)), dma((4,)), dma((4,)), dma((4,)), dma((4,)),
        ],
        compiler_params=pltpu.CompilerParams(
            collective_id=0, has_side_effects=True, vmem_limit_bytes=48 * 1024 * 1024
        ),
        cost_estimate=pl.CostEstimate(
            flops=3_900_000_000, bytes_accessed=9_000_000, transcendentals=1_000_000
        ),
    )(*(pltpu.with_memory_space_constraint(arg, pltpu.HBM) for arg in arrays))


def solution(mesh):
    return jax.shard_map(
        body,
        mesh=mesh,
        in_specs=(
            P("seq", "head"),
            P("seq", "head"),
            P("seq", "head"),
            P("seq", "head"),
            P("head", None),
        ),
        out_specs=P("seq", "head"),
        check_vma=False,
    )
```

```python
import functools

import jax
import jax.numpy as jnp
from jax import lax
from jax.experimental import pallas as pl
from jax.experimental.pallas import tpu as pltpu
from jax.sharding import PartitionSpec as P

HEADS = 32
HEAD_DIM = 128
F32 = jnp.float32
BF16 = jnp.bfloat16
MESH = pl.DeviceIdType.MESH

NX = 4
NZ = 8
STEPS = (2, 1, 3)
ROWS = 512
FEAT = 512
OUT = 768
PAIR = 256
NCHUNK = 4
HALF = OUT // 2


def sigmoid(value):
    return 0.5 + 0.5 * jnp.tanh(0.5 * value)


def silu(raw):
    value = raw.astype(F32)
    return (value * sigmoid(value)).astype(BF16)


def contract(lhs, rhs, lhs_dim, rhs_dim):
    return lax.dot_general(
        lhs, rhs, (((lhs_dim,), (rhs_dim,)), ((), ())), preferred_element_type=F32
    )


def kernel(
    q_hbm, k_hbm, v_hbm, g_hbm, w_hbm, out_ref,
    q_in, k_in, v_in, g_in, aq, ak, av, within, gate, squares,
    s_full, s_bf, sib, tot_bf, low_sum, arr_a, pay, arr_b, back, state,
    gathered, weight, acc, ss_own, ss_all,
    near, load_sem, z_send, z_recv, p_send, p_recv, a_send, a_recv, b_send, b_recv,
    ss_send, ss_recv, r_send, r_recv, l_send, l_recv,
    wa_send, wa_recv, wb_send, wb_recv, ws_send, ws_recv,
):
    seq = lax.axis_index("seq")
    z = lax.axis_index("head")
    c = lax.rem(seq, 2)
    x = lax.rem(lax.div(seq, 2), NX)
    y = lax.div(seq, 2 * NX)
    a = x * (1 - c) + y * c
    b = y * (1 - c) + x * c

    def chip(x_step, y_step):
        x2 = lax.rem(x + x_step, NX)
        y2 = lax.rem(y + y_step, NX)
        return ((y2 * NX + x2) * 2 + c, z)

    def a_peer(step):
        return chip(step * (1 - c), step * c)

    def b_peer(step):
        return chip(step * c, step * (1 - c))

    def z_peer(step):
        return (seq, lax.rem(z + step, NZ))

    sibling = (seq + 1 - 2 * c, z)

    def remote(src, dst, send_sem, recv_sem, device):
        return pltpu.make_async_remote_copy(
            src_ref=src, dst_ref=dst, send_sem=send_sem, recv_sem=recv_sem,
            device_id=device, device_id_type=MESH,
        )

    barrier = pltpu.get_barrier_semaphore()
    partners = (
        [sibling]
        + [chip(step, 0) for step in range(1, NX)]
        + [chip(0, step) for step in range(1, NX)]
        + [z_peer(1), z_peer(NZ - 1)]
    )
    for partner in partners:
        pl.semaphore_signal(barrier, inc=1, device_id=partner, device_id_type=MESH)

    def load(src, dst, index):
        copy = pltpu.make_async_copy(src, dst, load_sem.at[index])
        copy.start()
        return copy

    def head(h):
        return slice(h * HEAD_DIM, (h + 1) * HEAD_DIM)

    loads_kv = []
    for stage in range(2):
        part = pl.ds(stage * PAIR, PAIR)
        loads_kv.append((
            load(k_hbm.at[:, part], k_in.at[:, part], 2 * stage),
            load(v_hbm.at[:, part], v_in.at[:, part], 2 * stage + 1),
        ))

    def stage_heads(stage):
        return pl.ds(2 * stage, 2)

    def to_core1(stage):
        return remote(
            s_bf.at[stage_heads(stage)], sib.at[stage_heads(stage)],
            p_send.at[stage], p_recv.at[stage], sibling,
        )

    def to_core0(stage):
        return remote(
            back.at[stage_heads(stage)], state.at[stage_heads(stage)],
            p_send.at[2 + stage], p_recv.at[2 + stage], sibling,
        )

    def first_phase(h, step):
        index = h * (NX - 1) + step - 1
        device = chip(step, 0) if h % 2 == 0 else chip(0, step)
        return remote(
            tot_bf.at[h], arr_a.at[h, step - 1], a_send.at[index], a_recv.at[index], device
        )

    def second_phase(h, step):
        index = h * (NX - 1) + step - 1
        device = chip(0, step) if h % 2 == 0 else chip(step, 0)
        piece = 0 if h % 2 == 0 else lax.div(x + step, NX)
        return remote(
            pay.at[h, piece], arr_b.at[h, step - 1],
            b_send.at[index], b_recv.at[index], device,
        )

    def first_sends(h, step):
        if h % 2 == 0:
            return jnp.logical_or(x + step < NX, y < NX - 1)
        return y + step < NX

    def first_hears(h, step):
        if h % 2 == 0:
            return jnp.logical_or(x >= step, y < NX - 1)
        return y >= step

    def second_sends(h, step):
        if h % 2 == 0:
            return y + step < NX
        return jnp.logical_or(x + step < NX, y > 0)

    def second_hears(h, step):
        if h % 2 == 0:
            return y >= step
        return jnp.logical_or(x >= step, y > 0)

    def local_state(h):
        ak[:, head(h)] = silu(k_in[:, head(h)])
        av[:, head(h)] = silu(v_in[:, head(h)])
        outer = contract(ak[:, head(h)], av[:, head(h)], 0, 0)
        s_full[h] = outer
        s_bf[h] = outer.astype(BF16)

    def depart(stage):
        to_core1(stage).wait_recv()
        for h in (2 * stage, 2 * stage + 1):
            tot_bf[h] = (s_full[h] + sib[h].astype(F32)).astype(BF16)
            for step in STEPS:
                pl.when(first_sends(h, step))(first_phase(h, step).start)

    def greet(index, distance):
        for step in (distance, NZ - distance):
            pl.semaphore_signal(
                near.at[index], inc=1, device_id=z_peer(step), device_id_type=MESH
            )

    for copy in loads_kv[0]:
        copy.wait()
    load_q = load(q_hbm, q_in, 4)
    local_state(0)
    local_state(1)
    pl.semaphore_wait(barrier, len(partners))
    pl.when(c == 0)(lambda: to_core1(0).start())
    greet(0, 1)
    for copy in loads_kv[1]:
        copy.wait()
    load_g = load(g_hbm, g_in, 5)
    local_state(2)
    pl.when(c == 1)(lambda: depart(0))
    pl.semaphore_wait(near.at[0], 2)
    greet(1, 2)
    local_state(3)
    pl.when(c == 0)(lambda: to_core1(1).start())
    pl.when(c == 1)(lambda: depart(1))

    share = pl.multiple_of(c * 256 + b * 64 + a * 16, 16)
    pl.semaphore_wait(near.at[1], 2)
    weight_z = []
    for step in range(1, NZ):
        columns = pl.ds(pl.multiple_of(lax.rem(z + step, NZ) * OUT, 128), OUT)
        copy = remote(
            w_hbm.at[pl.ds(share, 16), columns],
            weight.at[NZ - step, pl.ds(share, 16)],
            z_send.at[step - 1], z_recv.at[step - 1], z_peer(step),
        )
        copy.start()
        weight_z.append(copy)

    half = ROWS // 2
    row_id = lax.broadcasted_iota(jnp.int32, (half, half), 0)
    col_id = lax.broadcasted_iota(jnp.int32, (half, half), 1)
    causal = row_id >= col_id

    def attend_block(h):
        for part in range(2):
            rows = slice(part * half, (part + 1) * half)
            qh = aq[rows, head(h)]
            diag = contract(qh, ak[rows, head(h)], 1, 1)
            diag = jnp.where(causal, diag, 0.0).astype(BF16)
            result = contract(diag, av[rows, head(h)], 1, 0)
            if part == 1:
                low = contract(qh, ak[0:half, head(h)], 1, 1).astype(BF16)
                result = result + contract(low, av[0:half, head(h)], 1, 0)
            within[rows, head(h)] = result

    load_q.wait()
    for h in range(4):
        aq[:, head(h)] = silu(q_in[:, head(h)])
    own_columns = pl.ds(pl.multiple_of(z * OUT, 128), OUT)
    load_w = load(w_hbm.at[:, own_columns], weight.at[0], 6)
    attend_block(0)
    attend_block(1)

    def add_term(copy, term, h):
        copy.wait_recv()
        low_sum[h] += term[...].astype(F32)

    def turn(stage):
        for h in (2 * stage, 2 * stage + 1):
            total = s_full[h] + sib[h].astype(F32)
            low_sum[h] = jnp.zeros((HEAD_DIM, HEAD_DIM), F32)
            if h % 2 == 0:
                pay[h, 0] = total.astype(BF16)

                @pl.when(y < NX - 1)
                def _(h=h, total=total):
                    lower = jnp.zeros((HEAD_DIM, HEAD_DIM), F32)
                    whole = total
                    for step in range(1, NX):
                        first_phase(h, step).wait_recv()
                        term = arr_a[h, step - 1].astype(F32)
                        lower = lower + term * jnp.where(x >= step, 1.0, 0.0).astype(F32)
                        whole = whole + term
                    low_sum[h] = lower
                    pay[h, 0] = whole.astype(BF16)

                @pl.when(y == NX - 1)
                def _(h=h):
                    for step in range(1, NX):
                        pl.when(x >= step)(functools.partial(
                            add_term, first_phase(h, step), arr_a.at[h, step - 1], h
                        ))
            else:
                for step in range(1, NX):
                    pl.when(first_hears(h, step))(functools.partial(
                        add_term, first_phase(h, step), arr_a.at[h, step - 1], h
                    ))
                pay[h, 0] = (low_sum[h] + total).astype(BF16)
                pay[h, 1] = low_sum[h].astype(BF16)
            for step in STEPS:
                pl.when(second_sends(h, step))(second_phase(h, step).start)

    pl.when(c == 1)(lambda: turn(0))
    attend_block(2)
    pl.when(c == 1)(lambda: turn(1))
    attend_block(3)
    load_g.wait()
    for h in range(4):
        gate[:, head(h)] = sigmoid(g_in[:, head(h)].astype(F32))

    def finish_state(stage):
        @pl.when(c == 1)
        def _():
            for h in (2 * stage, 2 * stage + 1):
                for step in range(1, NX):
                    pl.when(second_hears(h, step))(functools.partial(
                        add_term, second_phase(h, step), arr_b.at[h, step - 1], h
                    ))
                before = low_sum[h]
                back[h] = before.astype(BF16)
                state[h] = (before + sib[h].astype(F32)).astype(BF16)
            to_core0(stage).start()

        @pl.when(c == 0)
        def _():
            to_core0(stage).wait_recv()

    def slot_send(index, hop, chunk, up):
        part = lax.div(chunk, 2)
        rows = pl.ds(pl.multiple_of(lax.rem(chunk, 2) * half, half), half)
        if up:
            src, dst = lax.rem(NZ + 1 - hop, NZ), NZ - hop
            return remote(
                gathered.at[src, part, rows], gathered.at[dst, part, rows],
                r_send.at[index], r_recv.at[index], z_peer(1),
            )
        return remote(
            gathered.at[hop - 1, part, rows], gathered.at[hop, part, rows],
            l_send.at[index], l_recv.at[index], z_peer(NZ - 1),
        )

    def finish_attended(stage):
        for part in range(2):
            rows = slice(part * half, (part + 1) * half)
            total = jnp.zeros((half, HEAD_DIM), F32) if stage == 0 else squares[rows, :]
            for i in range(2):
                h = 2 * stage + i
                att = within[rows, head(h)] + contract(aq[rows, head(h)], state[h], 1, 0)
                total = total + att * att
                gathered[0, stage, rows, head(i)] = (att * gate[rows, head(h)]).astype(BF16)
            squares[rows, :] = total
            chunk = 2 * stage + part
            slot_send(chunk, 1, chunk, True).start()
            slot_send(chunk, 1, chunk, False).start()

    finish_state(0)
    finish_attended(0)
    finish_state(1)
    finish_attended(1)
    for group in range(ROWS // 128):
        tile = squares[group * 128 : (group + 1) * 128, :]
        ss_own[group : group + 1, :] = jnp.sum(tile.T, axis=0, keepdims=True)

    square_sends = []
    for step in range(1, NZ):
        copy = remote(
            ss_own, ss_all.at[step - 1], ss_send.at[step - 1], ss_recv.at[step - 1], z_peer(step)
        )
        copy.start()
        square_sends.append(copy)

    others = pl.ds(1, NZ - 1)

    def share_rows(step):
        return pl.ds(pl.multiple_of(c * 256 + b * 64 + lax.rem(a + step, NX) * 16, 16), 16)

    def group_rows(step):
        return pl.ds(pl.multiple_of(c * 256 + lax.rem(b + step, NX) * 64, 64), 64)

    def ring_starts(rows, peer, send_sem, recv_sem):
        piece = weight.at[others, rows(0)]
        up = remote(piece, piece, send_sem.at[0], recv_sem.at[0], peer(1))
        down = remote(piece, piece, send_sem.at[1], recv_sem.at[1], peer(NX - 1))
        up.start()
        down.start()
        return [up, down]

    def ring_forwards(rows, peer, send_sem, recv_sem, copies):
        copies[0].wait_recv()
        from_below = weight.at[others, rows(NX - 1), pl.ds(0, HALF)]
        up = remote(from_below, from_below, send_sem.at[2], recv_sem.at[2], peer(1))
        up.start()
        copies[1].wait_recv()
        from_above = weight.at[others, rows(1), pl.ds(HALF, HALF)]
        down = remote(from_above, from_above, send_sem.at[3], recv_sem.at[3], peer(NX - 1))
        down.start()
        return [up, down]


    def project(slot, row, count, fresh=False):
        rows = pl.ds(pl.multiple_of(row, 128), count)
        for n in range(OUT // 256):
            cols = slice(n * 256, (n + 1) * 256)
            term = contract(gathered[slot, 0, rows, :], weight[slot, 0:PAIR, cols], 1, 0)
            term = term + contract(gathered[slot, 1, rows, :], weight[slot, PAIR:FEAT, cols], 1, 0)
            if fresh:
                acc[rows, cols] = term
            else:
                acc[rows, cols] += term

    load_w.wait()
    for part in range(2):
        project(0, part * 256, 256, fresh=True)

    def pass_on(index, _):
        hop = lax.div(index, NCHUNK) + 1
        chunk = lax.rem(index, NCHUNK)
        slot_send(index, hop, chunk, True).wait_recv()
        slot_send(index + NCHUNK, hop + 1, chunk, True).start()
        slot_send(index, hop, chunk, False).wait_recv()
        slot_send(index + NCHUNK, hop + 1, chunk, False).start()
        return 0

    def pass_range(start, stop):
        lax.fori_loop(start, stop, pass_on, 0)

    for copy in weight_z:
        copy.wait_recv()
    ring_a = ring_starts(share_rows, a_peer, wa_send, wa_recv)
    pass_range(0, 1)
    ring_a2 = ring_forwards(share_rows, a_peer, wa_send, wa_recv, ring_a)
    pass_range(1, 2)
    for copy in ring_a2:
        copy.wait_recv()
    ring_b = ring_starts(group_rows, b_peer, wb_send, wb_recv)

    def to_sibling(step):
        piece = weight.at[others, group_rows(step)]
        copy = remote(piece, piece, ws_send.at[step], ws_recv.at[step], sibling)
        copy.start()
        return copy

    sibling_sends = [to_sibling(0)]
    pass_range(2, 5)
    ring_b2 = ring_forwards(group_rows, b_peer, wb_send, wb_recv, ring_b)
    sibling_sends.append(to_sibling(1))
    sibling_sends.append(to_sibling(3))
    pass_range(5, 8)
    for copy in ring_b2:
        copy.wait_recv()
    sibling_sends.append(to_sibling(2))
    for copy in sibling_sends:
        copy.wait_recv()

    def hop_three(chunk):
        index = 2 * NCHUNK + chunk
        slot_send(index, 3, chunk, True).wait_recv()
        if chunk < NCHUNK // 2:
            slot_send(index + NCHUNK, 4, chunk, True).start()
        slot_send(index, 3, chunk, False).wait_recv()
        if chunk >= NCHUNK // 2:
            slot_send(index + NCHUNK, 4, chunk, False).start()

    def project_whole(slot):
        def body(part, _):
            project(slot, part * 256, 256)
            return 0
        lax.fori_loop(0, 2, body, 0)

    hop_three(0)
    project_whole(7)
    hop_three(1)
    project_whole(1)
    hop_three(2)
    project_whole(6)
    hop_three(3)
    project_whole(2)
    project_whole(5)
    project_whole(3)

    for step in range(NZ - 1):
        square_sends[step].wait_recv()
    sums = ss_own[...]
    for step in range(NZ - 1):
        sums = sums + ss_all[step]
    factor = lax.rsqrt(sums / (HEADS * HEAD_DIM) + 1e-06)

    for part in range(2):
        slot_send(3 * NCHUNK + part, 4, part, True).wait_recv()
        slot_send(3 * NCHUNK + part + 2, 4, part + 2, False).wait_recv()
        project(4, part * half, half)
        for group in (2 * part, 2 * part + 1):
            rows = slice(group * 128, (group + 1) * 128)
            column = jnp.broadcast_to(factor[group : group + 1, :], (128, 128)).T
            for n in range(OUT // 128):
                cols = slice(n * 128, (n + 1) * 128)
                out_ref[rows, cols] = (acc[rows, cols] * column).astype(BF16)

    @pl.when(c == 0)
    def _():
        for stage in range(2):
            to_core1(stage).wait_send()

    @pl.when(c == 1)
    def _():
        for stage in range(2):
            to_core0(stage).wait_send()
        for h in range(4):
            for step in range(1, NX):
                pl.when(first_sends(h, step))(first_phase(h, step).wait_send)
                pl.when(second_sends(h, step))(second_phase(h, step).wait_send)

    for copy in (
        weight_z + square_sends + ring_a + ring_a2 + ring_b + ring_b2 + sibling_sends
    ):
        copy.wait_send()

    def drain(index, _):
        hop = lax.div(index, NCHUNK) + 1
        chunk = lax.rem(index, NCHUNK)
        slot_send(index, hop, chunk, True).wait_send()
        slot_send(index, hop, chunk, False).wait_send()
        return 0

    lax.fori_loop(0, 3 * NCHUNK, drain, 0)
    for chunk in range(NCHUNK):
        slot_send(3 * NCHUNK + chunk, 4, chunk, chunk < NCHUNK // 2).wait_send()


def body(*arrays):
    dma = pltpu.SemaphoreType.DMA
    full = (4, HEAD_DIM, HEAD_DIM)
    vmem = pltpu.VMEM
    return pl.pallas_call(
        kernel,
        out_shape=jax.ShapeDtypeStruct((ROWS, OUT), BF16),
        in_specs=[pl.BlockSpec(memory_space=pl.ANY)] * 5,
        out_specs=pl.BlockSpec(memory_space=pltpu.VMEM),
        scratch_shapes=[
            vmem((ROWS, FEAT), BF16), vmem((ROWS, FEAT), BF16),
            vmem((ROWS, FEAT), BF16), vmem((ROWS, FEAT), BF16),
            vmem((ROWS, FEAT), BF16), vmem((ROWS, FEAT), BF16), vmem((ROWS, FEAT), BF16),
            vmem((ROWS, FEAT), F32), vmem((ROWS, FEAT), F32), vmem((ROWS, HEAD_DIM), F32),
            vmem(full, F32), vmem(full, BF16), vmem(full, BF16), vmem(full, BF16), vmem(full, F32),
            vmem((4, NX - 1, HEAD_DIM, HEAD_DIM), BF16), vmem((4, 2, HEAD_DIM, HEAD_DIM), BF16),
            vmem((4, NX - 1, HEAD_DIM, HEAD_DIM), BF16), vmem(full, BF16), vmem(full, BF16),
            vmem((NZ, 2, ROWS, PAIR), BF16), vmem((NZ, ROWS, OUT), BF16),
            vmem((ROWS, OUT), F32), vmem((4, 128), F32), vmem((NZ - 1, 4, 128), F32),
            pltpu.SemaphoreType.REGULAR((2,)), dma((7,)), dma((NZ - 1,)), dma((NZ - 1,)), dma((4,)), dma((4,)),
            dma((12,)), dma((12,)), dma((12,)), dma((12,)),
            dma((NZ - 1,)), dma((NZ - 1,)),
            dma((4 * NCHUNK,)), dma((4 * NCHUNK,)), dma((4 * NCHUNK,)), dma((4 * NCHUNK,)),
            dma((4,)), dma((4,)), dma((4,)), dma((4,)), dma((4,)), dma((4,)),
        ],
        compiler_params=pltpu.CompilerParams(
            collective_id=0, has_side_effects=True, vmem_limit_bytes=48 * 1024 * 1024
        ),
        cost_estimate=pl.CostEstimate(
            flops=3_900_000_000, bytes_accessed=9_000_000, transcendentals=1_000_000
        ),
    )(*(pltpu.with_memory_space_constraint(arg, pltpu.HBM) for arg in arrays))


def solution(mesh):
    return jax.shard_map(
        body,
        mesh=mesh,
        in_specs=(
            P("seq", "head"),
            P("seq", "head"),
            P("seq", "head"),
            P("seq", "head"),
            P("head", None),
        ),
        out_specs=P("seq", "head"),
        check_vma=False,
    )
```

```python
import functools

import jax
import jax.numpy as jnp
from jax import lax
from jax.experimental import pallas as pl
from jax.experimental.pallas import tpu as pltpu
from jax.sharding import PartitionSpec as P

HEADS = 32
HEAD_DIM = 128
F32 = jnp.float32
BF16 = jnp.bfloat16
MESH = pl.DeviceIdType.MESH

NX = 4
NZ = 8
STEPS = (2, 1, 3)
ROWS = 512
FEAT = 512
OUT = 768
PAIR = 256
NCHUNK = 4
HALF = OUT // 2


def sigmoid(value):
    return 0.5 + 0.5 * jnp.tanh(0.5 * value)


def silu(raw):
    value = raw.astype(F32)
    return (value * sigmoid(value)).astype(BF16)


def contract(lhs, rhs, lhs_dim, rhs_dim):
    return lax.dot_general(
        lhs, rhs, (((lhs_dim,), (rhs_dim,)), ((), ())), preferred_element_type=F32
    )


def kernel(
    q_hbm, k_hbm, v_hbm, g_hbm, w_hbm, out_ref,
    q_in, k_in, v_in, g_in, aq, ak, av, within, gate, squares,
    s_full, s_bf, sib, tot_bf, low_sum, arr_a, pay, arr_b, back, state,
    gathered, weight, acc, ss_own, ss_all,
    near, load_sem, z_send, z_recv, p_send, p_recv, a_send, a_recv, b_send, b_recv,
    ss_send, ss_recv, r_send, r_recv, l_send, l_recv,
    wa_send, wa_recv, wb_send, wb_recv, ws_send, ws_recv,
):
    seq = lax.axis_index("seq")
    z = lax.axis_index("head")
    c = lax.rem(seq, 2)
    x = lax.rem(lax.div(seq, 2), NX)
    y = lax.div(seq, 2 * NX)
    a = x * (1 - c) + y * c
    b = y * (1 - c) + x * c

    def chip(x_step, y_step):
        x2 = lax.rem(x + x_step, NX)
        y2 = lax.rem(y + y_step, NX)
        return ((y2 * NX + x2) * 2 + c, z)

    def a_peer(step):
        return chip(step * (1 - c), step * c)

    def b_peer(step):
        return chip(step * c, step * (1 - c))

    def z_peer(step):
        return (seq, lax.rem(z + step, NZ))

    sibling = (seq + 1 - 2 * c, z)

    def remote(src, dst, send_sem, recv_sem, device):
        return pltpu.make_async_remote_copy(
            src_ref=src, dst_ref=dst, send_sem=send_sem, recv_sem=recv_sem,
            device_id=device, device_id_type=MESH,
        )

    barrier = pltpu.get_barrier_semaphore()
    partners = (
        [sibling]
        + [chip(step, 0) for step in range(1, NX)]
        + [chip(0, step) for step in range(1, NX)]
        + [z_peer(1), z_peer(NZ - 1)]
    )
    for partner in partners:
        pl.semaphore_signal(barrier, inc=1, device_id=partner, device_id_type=MESH)

    def load(src, dst, index):
        copy = pltpu.make_async_copy(src, dst, load_sem.at[index])
        copy.start()
        return copy

    def head(h):
        return slice(h * HEAD_DIM, (h + 1) * HEAD_DIM)

    loads_kv = []
    for stage in range(2):
        part = pl.ds(stage * PAIR, PAIR)
        loads_kv.append((
            load(k_hbm.at[:, part], k_in.at[:, part], 2 * stage),
            load(v_hbm.at[:, part], v_in.at[:, part], 2 * stage + 1),
        ))

    def stage_heads(stage):
        return pl.ds(2 * stage, 2)

    def to_core1(stage):
        return remote(
            s_bf.at[stage_heads(stage)], sib.at[stage_heads(stage)],
            p_send.at[stage], p_recv.at[stage], sibling,
        )

    def to_core0(stage):
        return remote(
            back.at[stage_heads(stage)], state.at[stage_heads(stage)],
            p_send.at[2 + stage], p_recv.at[2 + stage], sibling,
        )

    def first_phase(h, step):
        index = h * (NX - 1) + step - 1
        device = chip(step, 0) if h % 2 == 0 else chip(0, step)
        return remote(
            tot_bf.at[h], arr_a.at[h, step - 1], a_send.at[index], a_recv.at[index], device
        )

    def second_phase(h, step):
        index = h * (NX - 1) + step - 1
        device = chip(0, step) if h % 2 == 0 else chip(step, 0)
        piece = 0 if h % 2 == 0 else lax.div(x + step, NX)
        return remote(
            pay.at[h, piece], arr_b.at[h, step - 1],
            b_send.at[index], b_recv.at[index], device,
        )

    def first_sends(h, step):
        if h % 2 == 0:
            return jnp.logical_or(x + step < NX, y < NX - 1)
        return y + step < NX

    def first_hears(h, step):
        if h % 2 == 0:
            return jnp.logical_or(x >= step, y < NX - 1)
        return y >= step

    def second_sends(h, step):
        if h % 2 == 0:
            return y + step < NX
        return jnp.logical_or(x + step < NX, y > 0)

    def second_hears(h, step):
        if h % 2 == 0:
            return y >= step
        return jnp.logical_or(x >= step, y > 0)

    def local_state(h):
        ak[:, head(h)] = silu(k_in[:, head(h)])
        av[:, head(h)] = silu(v_in[:, head(h)])
        outer = contract(ak[:, head(h)], av[:, head(h)], 0, 0)
        s_full[h] = outer
        s_bf[h] = outer.astype(BF16)

    def depart(stage):
        to_core1(stage).wait_recv()
        for h in (2 * stage, 2 * stage + 1):
            tot_bf[h] = (s_full[h] + sib[h].astype(F32)).astype(BF16)
            for step in STEPS:
                pl.when(first_sends(h, step))(first_phase(h, step).start)

    def greet(index, distance):
        for step in (distance, NZ - distance):
            pl.semaphore_signal(
                near.at[index], inc=1, device_id=z_peer(step), device_id_type=MESH
            )

    for copy in loads_kv[0]:
        copy.wait()
    load_q = load(q_hbm, q_in, 4)
    local_state(0)
    local_state(1)
    pl.semaphore_wait(barrier, len(partners))
    pl.when(c == 0)(lambda: to_core1(0).start())
    greet(0, 1)
    for copy in loads_kv[1]:
        copy.wait()
    load_g = load(g_hbm, g_in, 5)
    local_state(2)
    pl.when(c == 1)(lambda: depart(0))
    pl.semaphore_wait(near.at[0], 2)
    greet(1, 2)
    local_state(3)
    pl.when(c == 0)(lambda: to_core1(1).start())
    pl.when(c == 1)(lambda: depart(1))

    share = pl.multiple_of(c * 256 + b * 64 + a * 16, 16)
    pl.semaphore_wait(near.at[1], 2)
    weight_z = []
    for step in range(1, NZ):
        columns = pl.ds(pl.multiple_of(lax.rem(z + step, NZ) * OUT, 128), OUT)
        copy = remote(
            w_hbm.at[pl.ds(share, 16), columns],
            weight.at[NZ - step, pl.ds(share, 16)],
            z_send.at[step - 1], z_recv.at[step - 1], z_peer(step),
        )
        copy.start()
        weight_z.append(copy)

    half = ROWS // 2
    row_id = lax.broadcasted_iota(jnp.int32, (half, half), 0)
    col_id = lax.broadcasted_iota(jnp.int32, (half, half), 1)
    causal = row_id >= col_id

    def attend_block(h):
        for part in range(2):
            rows = slice(part * half, (part + 1) * half)
            qh = aq[rows, head(h)]
            diag = contract(qh, ak[rows, head(h)], 1, 1)
            diag = jnp.where(causal, diag, 0.0).astype(BF16)
            result = contract(diag, av[rows, head(h)], 1, 0)
            if part == 1:
                low = contract(qh, ak[0:half, head(h)], 1, 1).astype(BF16)
                result = result + contract(low, av[0:half, head(h)], 1, 0)
            within[rows, head(h)] = result

    load_q.wait()
    for h in range(4):
        aq[:, head(h)] = silu(q_in[:, head(h)])
    own_columns = pl.ds(pl.multiple_of(z * OUT, 128), OUT)
    load_w = load(w_hbm.at[:, own_columns], weight.at[0], 6)
    attend_block(0)

    def add_term(copy, term, h):
        copy.wait_recv()
        low_sum[h] += term[...].astype(F32)

    def turn(stage):
        for h in (2 * stage, 2 * stage + 1):
            total = s_full[h] + sib[h].astype(F32)
            low_sum[h] = jnp.zeros((HEAD_DIM, HEAD_DIM), F32)
            if h % 2 == 0:
                pay[h, 0] = total.astype(BF16)

                @pl.when(y < NX - 1)
                def _(h=h, total=total):
                    lower = jnp.zeros((HEAD_DIM, HEAD_DIM), F32)
                    whole = total
                    for step in range(1, NX):
                        first_phase(h, step).wait_recv()
                        term = arr_a[h, step - 1].astype(F32)
                        lower = lower + term * jnp.where(x >= step, 1.0, 0.0).astype(F32)
                        whole = whole + term
                    low_sum[h] = lower
                    pay[h, 0] = whole.astype(BF16)

                @pl.when(y == NX - 1)
                def _(h=h):
                    for step in range(1, NX):
                        pl.when(x >= step)(functools.partial(
                            add_term, first_phase(h, step), arr_a.at[h, step - 1], h
                        ))
            else:
                for step in range(1, NX):
                    pl.when(first_hears(h, step))(functools.partial(
                        add_term, first_phase(h, step), arr_a.at[h, step - 1], h
                    ))
                pay[h, 0] = (low_sum[h] + total).astype(BF16)
                pay[h, 1] = low_sum[h].astype(BF16)
            for step in STEPS:
                pl.when(second_sends(h, step))(second_phase(h, step).start)

    pl.when(c == 1)(lambda: turn(0))
    attend_block(1)
    attend_block(2)
    pl.when(c == 1)(lambda: turn(1))
    attend_block(3)
    load_g.wait()
    for h in range(4):
        gate[:, head(h)] = sigmoid(g_in[:, head(h)].astype(F32))

    def finish_state(stage):
        @pl.when(c == 1)
        def _():
            for h in (2 * stage, 2 * stage + 1):
                for step in range(1, NX):
                    pl.when(second_hears(h, step))(functools.partial(
                        add_term, second_phase(h, step), arr_b.at[h, step - 1], h
                    ))
                before = low_sum[h]
                back[h] = before.astype(BF16)
                state[h] = (before + sib[h].astype(F32)).astype(BF16)
            to_core0(stage).start()

        @pl.when(c == 0)
        def _():
            to_core0(stage).wait_recv()

    def slot_send(index, hop, chunk, up):
        part = lax.div(chunk, 2)
        rows = pl.ds(pl.multiple_of(lax.rem(chunk, 2) * half, half), half)
        if up:
            src, dst = lax.rem(NZ + 1 - hop, NZ), NZ - hop
            return remote(
                gathered.at[src, part, rows], gathered.at[dst, part, rows],
                r_send.at[index], r_recv.at[index], z_peer(1),
            )
        return remote(
            gathered.at[hop - 1, part, rows], gathered.at[hop, part, rows],
            l_send.at[index], l_recv.at[index], z_peer(NZ - 1),
        )

    def finish_attended(stage):
        for part in range(2):
            rows = slice(part * half, (part + 1) * half)
            total = jnp.zeros((half, HEAD_DIM), F32) if stage == 0 else squares[rows, :]
            for i in range(2):
                h = 2 * stage + i
                att = within[rows, head(h)] + contract(aq[rows, head(h)], state[h], 1, 0)
                total = total + att * att
                gathered[0, stage, rows, head(i)] = (att * gate[rows, head(h)]).astype(BF16)
            squares[rows, :] = total
            chunk = 2 * stage + part
            slot_send(chunk, 1, chunk, True).start()
            slot_send(chunk, 1, chunk, False).start()

    finish_state(0)
    finish_attended(0)
    finish_state(1)
    finish_attended(1)
    for group in range(ROWS // 128):
        tile = squares[group * 128 : (group + 1) * 128, :]
        ss_own[group : group + 1, :] = jnp.sum(tile.T, axis=0, keepdims=True)

    square_sends = []
    for step in range(1, NZ):
        copy = remote(
            ss_own, ss_all.at[step - 1], ss_send.at[step - 1], ss_recv.at[step - 1], z_peer(step)
        )
        copy.start()
        square_sends.append(copy)

    others = pl.ds(1, NZ - 1)

    def share_rows(step):
        return pl.ds(pl.multiple_of(c * 256 + b * 64 + lax.rem(a + step, NX) * 16, 16), 16)

    def group_rows(step):
        return pl.ds(pl.multiple_of(c * 256 + lax.rem(b + step, NX) * 64, 64), 64)

    def ring_starts(rows, peer, send_sem, recv_sem):
        piece = weight.at[others, rows(0)]
        up = remote(piece, piece, send_sem.at[0], recv_sem.at[0], peer(1))
        down = remote(piece, piece, send_sem.at[1], recv_sem.at[1], peer(NX - 1))
        up.start()
        down.start()
        return [up, down]

    def ring_forwards(rows, peer, send_sem, recv_sem, copies):
        copies[0].wait_recv()
        from_below = weight.at[others, rows(NX - 1), pl.ds(0, HALF)]
        up = remote(from_below, from_below, send_sem.at[2], recv_sem.at[2], peer(1))
        up.start()
        copies[1].wait_recv()
        from_above = weight.at[others, rows(1), pl.ds(HALF, HALF)]
        down = remote(from_above, from_above, send_sem.at[3], recv_sem.at[3], peer(NX - 1))
        down.start()
        return [up, down]


    def project(slot, row, count, fresh=False):
        rows = pl.ds(pl.multiple_of(row, 128), count)
        for n in range(OUT // 256):
            cols = slice(n * 256, (n + 1) * 256)
            term = contract(gathered[slot, 0, rows, :], weight[slot, 0:PAIR, cols], 1, 0)
            term = term + contract(gathered[slot, 1, rows, :], weight[slot, PAIR:FEAT, cols], 1, 0)
            if fresh:
                acc[rows, cols] = term
            else:
                acc[rows, cols] += term

    load_w.wait()
    for part in range(2):
        project(0, part * 256, 256, fresh=True)

    def pass_on(index, _):
        hop = lax.div(index, NCHUNK) + 1
        chunk = lax.rem(index, NCHUNK)
        slot_send(index, hop, chunk, True).wait_recv()
        slot_send(index + NCHUNK, hop + 1, chunk, True).start()
        slot_send(index, hop, chunk, False).wait_recv()
        slot_send(index + NCHUNK, hop + 1, chunk, False).start()
        return 0

    def pass_range(start, stop):
        lax.fori_loop(start, stop, pass_on, 0)

    for copy in weight_z:
        copy.wait_recv()
    ring_a = ring_starts(share_rows, a_peer, wa_send, wa_recv)
    pass_range(0, 1)
    ring_a2 = ring_forwards(share_rows, a_peer, wa_send, wa_recv, ring_a)
    pass_range(1, 2)
    for copy in ring_a2:
        copy.wait_recv()
    ring_b = ring_starts(group_rows, b_peer, wb_send, wb_recv)

    def to_sibling(step):
        piece = weight.at[others, group_rows(step)]
        copy = remote(piece, piece, ws_send.at[step], ws_recv.at[step], sibling)
        copy.start()
        return copy

    sibling_sends = [to_sibling(0)]
    pass_range(2, 5)
    ring_b2 = ring_forwards(group_rows, b_peer, wb_send, wb_recv, ring_b)
    sibling_sends.append(to_sibling(1))
    sibling_sends.append(to_sibling(3))
    pass_range(5, 8)
    for copy in ring_b2:
        copy.wait_recv()
    sibling_sends.append(to_sibling(2))
    for copy in sibling_sends:
        copy.wait_recv()

    def last_hop(unit, up):
        chunk = unit // 2
        rows = pl.ds((chunk % 2) * half + (unit % 2) * 128, 128)
        src, sends, recvs, device = (
            (5, r_send, r_recv, z_peer(1)) if up else (3, l_send, l_recv, z_peer(NZ - 1))
        )
        index = 3 * NCHUNK + unit
        return remote(
            gathered.at[src, chunk // 2, rows], gathered.at[4, chunk // 2, rows],
            sends.at[index], recvs.at[index], device,
        )

    def hop_three(chunk):
        index = 2 * NCHUNK + chunk
        units = (2 * chunk, 2 * chunk + 1)
        up = units[1] < NCHUNK
        slot_send(index, 3, chunk, True).wait_recv()
        if up:
            for unit in units:
                last_hop(unit, True).start()
        slot_send(index, 3, chunk, False).wait_recv()
        if not up:
            for unit in units:
                last_hop(unit, False).start()

    def project_whole(slot):
        def body(part, _):
            project(slot, part * 256, 256)
            return 0
        lax.fori_loop(0, 2, body, 0)

    hop_three(0)
    project_whole(7)
    hop_three(1)
    project_whole(1)
    hop_three(2)
    project_whole(6)
    hop_three(3)
    project_whole(2)
    project_whole(5)
    project_whole(3)

    for step in range(NZ - 1):
        square_sends[step].wait_recv()
    sums = ss_own[...]
    for step in range(NZ - 1):
        sums = sums + ss_all[step]
    factor = lax.rsqrt(sums / (HEADS * HEAD_DIM) + 1e-06)

    for group in range(ROWS // 128):
        last_hop(group, True).wait_recv()
        last_hop(group + NCHUNK, False).wait_recv()
        project(4, group * 128, 128)
        rows = slice(group * 128, (group + 1) * 128)
        column = jnp.broadcast_to(factor[group : group + 1, :], (128, 128)).T
        for n in range(OUT // 128):
            cols = slice(n * 128, (n + 1) * 128)
            out_ref[rows, cols] = (acc[rows, cols] * column).astype(BF16)

    @pl.when(c == 0)
    def _():
        for stage in range(2):
            to_core1(stage).wait_send()

    @pl.when(c == 1)
    def _():
        for stage in range(2):
            to_core0(stage).wait_send()
        for h in range(4):
            for step in range(1, NX):
                pl.when(first_sends(h, step))(first_phase(h, step).wait_send)
                pl.when(second_sends(h, step))(second_phase(h, step).wait_send)

    for copy in (
        weight_z + square_sends + ring_a + ring_a2 + ring_b + ring_b2 + sibling_sends
    ):
        copy.wait_send()

    def drain(index, _):
        hop = lax.div(index, NCHUNK) + 1
        chunk = lax.rem(index, NCHUNK)
        slot_send(index, hop, chunk, True).wait_send()
        slot_send(index, hop, chunk, False).wait_send()
        return 0

    lax.fori_loop(0, 3 * NCHUNK, drain, 0)
    for unit in range(2 * NCHUNK):
        last_hop(unit, unit < NCHUNK).wait_send()


def body(*arrays):
    dma = pltpu.SemaphoreType.DMA
    full = (4, HEAD_DIM, HEAD_DIM)
    vmem = pltpu.VMEM
    return pl.pallas_call(
        kernel,
        out_shape=jax.ShapeDtypeStruct((ROWS, OUT), BF16),
        in_specs=[pl.BlockSpec(memory_space=pl.ANY)] * 5,
        out_specs=pl.BlockSpec(memory_space=pltpu.VMEM),
        scratch_shapes=[
            vmem((ROWS, FEAT), BF16), vmem((ROWS, FEAT), BF16),
            vmem((ROWS, FEAT), BF16), vmem((ROWS, FEAT), BF16),
            vmem((ROWS, FEAT), BF16), vmem((ROWS, FEAT), BF16), vmem((ROWS, FEAT), BF16),
            vmem((ROWS, FEAT), F32), vmem((ROWS, FEAT), F32), vmem((ROWS, HEAD_DIM), F32),
            vmem(full, F32), vmem(full, BF16), vmem(full, BF16), vmem(full, BF16), vmem(full, F32),
            vmem((4, NX - 1, HEAD_DIM, HEAD_DIM), BF16), vmem((4, 2, HEAD_DIM, HEAD_DIM), BF16),
            vmem((4, NX - 1, HEAD_DIM, HEAD_DIM), BF16), vmem(full, BF16), vmem(full, BF16),
            vmem((NZ, 2, ROWS, PAIR), BF16), vmem((NZ, ROWS, OUT), BF16),
            vmem((ROWS, OUT), F32), vmem((4, 128), F32), vmem((NZ - 1, 4, 128), F32),
            pltpu.SemaphoreType.REGULAR((2,)), dma((7,)), dma((NZ - 1,)), dma((NZ - 1,)), dma((4,)), dma((4,)),
            dma((12,)), dma((12,)), dma((12,)), dma((12,)),
            dma((NZ - 1,)), dma((NZ - 1,)),
            dma((5 * NCHUNK,)), dma((5 * NCHUNK,)), dma((5 * NCHUNK,)), dma((5 * NCHUNK,)),
            dma((4,)), dma((4,)), dma((4,)), dma((4,)), dma((4,)), dma((4,)),
        ],
        compiler_params=pltpu.CompilerParams(
            collective_id=0, has_side_effects=True, vmem_limit_bytes=48 * 1024 * 1024
        ),
        cost_estimate=pl.CostEstimate(
            flops=3_900_000_000, bytes_accessed=9_000_000, transcendentals=1_000_000
        ),
    )(*(pltpu.with_memory_space_constraint(arg, pltpu.HBM) for arg in arrays))


def solution(mesh):
    return jax.shard_map(
        body,
        mesh=mesh,
        in_specs=(
            P("seq", "head"),
            P("seq", "head"),
            P("seq", "head"),
            P("seq", "head"),
            P("head", None),
        ),
        out_specs=P("seq", "head"),
        check_vma=False,
    )
```

```python
import functools

import jax
import jax.numpy as jnp
from jax import lax
from jax.experimental import pallas as pl
from jax.experimental.pallas import tpu as pltpu
from jax.sharding import PartitionSpec as P

HEADS = 32
HEAD_DIM = 128
F32 = jnp.float32
BF16 = jnp.bfloat16
MESH = pl.DeviceIdType.MESH

NX = 4
NZ = 8
STEPS = (2, 1, 3)
ROWS = 512
FEAT = 512
OUT = 768
PAIR = 256
NCHUNK = 4
HALF = OUT // 2


def sigmoid(value):
    return 0.5 + 0.5 * jnp.tanh(0.5 * value)


def silu(raw):
    value = raw.astype(F32)
    return (value * sigmoid(value)).astype(BF16)


def contract(lhs, rhs, lhs_dim, rhs_dim):
    return lax.dot_general(
        lhs, rhs, (((lhs_dim,), (rhs_dim,)), ((), ())), preferred_element_type=F32
    )


def kernel(
    q_hbm, k_hbm, v_hbm, g_hbm, w_hbm, out_ref,
    q_in, k_in, v_in, g_in, aq, ak, av, within, gate, squares,
    s_full, s_bf, sib, tot_bf, low_sum, arr_a, pay, arr_b, back, state,
    gathered, weight, acc, ss_own, ss_all,
    near, load_sem, z_send, z_recv, p_send, p_recv, a_send, a_recv, b_send, b_recv,
    ss_send, ss_recv, r_send, r_recv, l_send, l_recv,
    wa_send, wa_recv, wb_send, wb_recv, ws_send, ws_recv,
):
    seq = lax.axis_index("seq")
    z = lax.axis_index("head")
    c = lax.rem(seq, 2)
    x = lax.rem(lax.div(seq, 2), NX)
    y = lax.div(seq, 2 * NX)
    a = x * (1 - c) + y * c
    b = y * (1 - c) + x * c

    def chip(x_step, y_step):
        x2 = lax.rem(x + x_step, NX)
        y2 = lax.rem(y + y_step, NX)
        return ((y2 * NX + x2) * 2 + c, z)

    def a_peer(step):
        return chip(step * (1 - c), step * c)

    def b_peer(step):
        return chip(step * c, step * (1 - c))

    def z_peer(step):
        return (seq, lax.rem(z + step, NZ))

    sibling = (seq + 1 - 2 * c, z)

    def remote(src, dst, send_sem, recv_sem, device):
        return pltpu.make_async_remote_copy(
            src_ref=src, dst_ref=dst, send_sem=send_sem, recv_sem=recv_sem,
            device_id=device, device_id_type=MESH,
        )

    barrier = pltpu.get_barrier_semaphore()
    partners = (
        [sibling]
        + [chip(step, 0) for step in range(1, NX)]
        + [chip(0, step) for step in range(1, NX)]
        + [z_peer(1), z_peer(NZ - 1)]
    )
    for partner in partners:
        pl.semaphore_signal(barrier, inc=1, device_id=partner, device_id_type=MESH)

    def load(src, dst, index):
        copy = pltpu.make_async_copy(src, dst, load_sem.at[index])
        copy.start()
        return copy

    def head(h):
        return slice(h * HEAD_DIM, (h + 1) * HEAD_DIM)

    loads_kv = []
    for stage in range(2):
        part = pl.ds(stage * PAIR, PAIR)
        loads_kv.append((
            load(k_hbm.at[:, part], k_in.at[:, part], 2 * stage),
            load(v_hbm.at[:, part], v_in.at[:, part], 2 * stage + 1),
        ))

    def stage_heads(stage):
        return pl.ds(2 * stage, 2)

    def to_core1(h):
        return remote(s_bf.at[h], sib.at[h], p_send.at[h], p_recv.at[h], sibling)

    def to_core0(stage):
        return remote(
            back.at[stage_heads(stage)], state.at[stage_heads(stage)],
            p_send.at[4 + stage], p_recv.at[4 + stage], sibling,
        )

    def first_phase(h, step):
        index = h * (NX - 1) + step - 1
        device = chip(step, 0) if h % 2 == 0 else chip(0, step)
        return remote(
            tot_bf.at[h], arr_a.at[h, step - 1], a_send.at[index], a_recv.at[index], device
        )

    def second_phase(h, step):
        index = h * (NX - 1) + step - 1
        device = chip(0, step) if h % 2 == 0 else chip(step, 0)
        piece = 0 if h % 2 == 0 else lax.div(x + step, NX)
        return remote(
            pay.at[h, piece], arr_b.at[h, step - 1],
            b_send.at[index], b_recv.at[index], device,
        )

    def first_sends(h, step):
        if h % 2 == 0:
            return jnp.logical_or(x + step < NX, y < NX - 1)
        return y + step < NX

    def first_hears(h, step):
        if h % 2 == 0:
            return jnp.logical_or(x >= step, y < NX - 1)
        return y >= step

    def second_sends(h, step):
        if h % 2 == 0:
            return y + step < NX
        return jnp.logical_or(x + step < NX, y > 0)

    def second_hears(h, step):
        if h % 2 == 0:
            return y >= step
        return jnp.logical_or(x >= step, y > 0)

    def local_state(h):
        ak[:, head(h)] = silu(k_in[:, head(h)])
        av[:, head(h)] = silu(v_in[:, head(h)])
        outer = contract(ak[:, head(h)], av[:, head(h)], 0, 0)
        s_full[h] = outer
        s_bf[h] = outer.astype(BF16)

    def depart(stage):
        for h in (2 * stage, 2 * stage + 1):
            to_core1(h).wait_recv()
            tot_bf[h] = (s_full[h] + sib[h].astype(F32)).astype(BF16)
            for step in STEPS:
                pl.when(first_sends(h, step))(first_phase(h, step).start)

    def greet(index, distance):
        for step in (distance, NZ - distance):
            pl.semaphore_signal(
                near.at[index], inc=1, device_id=z_peer(step), device_id_type=MESH
            )

    for copy in loads_kv[0]:
        copy.wait()
    load_q = load(q_hbm, q_in, 4)
    local_state(0)
    pl.semaphore_wait(barrier, len(partners))
    pl.when(c == 0)(lambda: to_core1(0).start())
    greet(0, 1)
    local_state(1)
    pl.when(c == 0)(lambda: to_core1(1).start())
    for copy in loads_kv[1]:
        copy.wait()
    load_g = load(g_hbm, g_in, 5)
    local_state(2)
    pl.when(c == 0)(lambda: to_core1(2).start())
    pl.when(c == 1)(lambda: depart(0))
    pl.semaphore_wait(near.at[0], 2)
    greet(1, 2)
    local_state(3)
    pl.when(c == 0)(lambda: to_core1(3).start())
    pl.when(c == 1)(lambda: depart(1))

    share = pl.multiple_of(c * 256 + b * 64 + a * 16, 16)
    pl.semaphore_wait(near.at[1], 2)
    weight_z = []
    for step in range(1, NZ):
        columns = pl.ds(pl.multiple_of(lax.rem(z + step, NZ) * OUT, 128), OUT)
        copy = remote(
            w_hbm.at[pl.ds(share, 16), columns],
            weight.at[NZ - step, pl.ds(share, 16)],
            z_send.at[step - 1], z_recv.at[step - 1], z_peer(step),
        )
        copy.start()
        weight_z.append(copy)

    half = ROWS // 2
    row_id = lax.broadcasted_iota(jnp.int32, (half, half), 0)
    col_id = lax.broadcasted_iota(jnp.int32, (half, half), 1)
    causal = row_id >= col_id

    def attend_block(h):
        for part in range(2):
            rows = slice(part * half, (part + 1) * half)
            qh = aq[rows, head(h)]
            diag = contract(qh, ak[rows, head(h)], 1, 1)
            diag = jnp.where(causal, diag, 0.0).astype(BF16)
            result = contract(diag, av[rows, head(h)], 1, 0)
            if part == 1:
                low = contract(qh, ak[0:half, head(h)], 1, 1).astype(BF16)
                result = result + contract(low, av[0:half, head(h)], 1, 0)
            within[rows, head(h)] = result

    load_q.wait()
    for h in range(4):
        aq[:, head(h)] = silu(q_in[:, head(h)])
    own_columns = pl.ds(pl.multiple_of(z * OUT, 128), OUT)
    load_w = load(w_hbm.at[:, own_columns], weight.at[0], 6)
    attend_block(0)

    def add_term(copy, term, h):
        copy.wait_recv()
        low_sum[h] += term[...].astype(F32)

    def turn(stage):
        for h in (2 * stage, 2 * stage + 1):
            total = s_full[h] + sib[h].astype(F32)
            low_sum[h] = jnp.zeros((HEAD_DIM, HEAD_DIM), F32)
            if h % 2 == 0:
                pay[h, 0] = total.astype(BF16)

                @pl.when(y < NX - 1)
                def _(h=h, total=total):
                    lower = jnp.zeros((HEAD_DIM, HEAD_DIM), F32)
                    whole = total
                    for step in range(1, NX):
                        first_phase(h, step).wait_recv()
                        term = arr_a[h, step - 1].astype(F32)
                        lower = lower + term * jnp.where(x >= step, 1.0, 0.0).astype(F32)
                        whole = whole + term
                    low_sum[h] = lower
                    pay[h, 0] = whole.astype(BF16)

                @pl.when(y == NX - 1)
                def _(h=h):
                    for step in range(1, NX):
                        pl.when(x >= step)(functools.partial(
                            add_term, first_phase(h, step), arr_a.at[h, step - 1], h
                        ))
            else:
                for step in range(1, NX):
                    pl.when(first_hears(h, step))(functools.partial(
                        add_term, first_phase(h, step), arr_a.at[h, step - 1], h
                    ))
                pay[h, 0] = (low_sum[h] + total).astype(BF16)
                pay[h, 1] = low_sum[h].astype(BF16)
            for step in STEPS:
                pl.when(second_sends(h, step))(second_phase(h, step).start)

    pl.when(c == 1)(lambda: turn(0))
    attend_block(1)
    attend_block(2)
    pl.when(c == 1)(lambda: turn(1))
    attend_block(3)
    load_g.wait()
    for h in range(4):
        gate[:, head(h)] = sigmoid(g_in[:, head(h)].astype(F32))

    def finish_state(stage):
        @pl.when(c == 1)
        def _():
            for h in (2 * stage, 2 * stage + 1):
                for step in range(1, NX):
                    pl.when(second_hears(h, step))(functools.partial(
                        add_term, second_phase(h, step), arr_b.at[h, step - 1], h
                    ))
                before = low_sum[h]
                back[h] = before.astype(BF16)
                state[h] = (before + sib[h].astype(F32)).astype(BF16)
            to_core0(stage).start()

        @pl.when(c == 0)
        def _():
            to_core0(stage).wait_recv()

    def slot_send(index, hop, chunk, up):
        part = lax.div(chunk, 2)
        rows = pl.ds(pl.multiple_of(lax.rem(chunk, 2) * half, half), half)
        if up:
            src, dst = lax.rem(NZ + 1 - hop, NZ), NZ - hop
            return remote(
                gathered.at[src, part, rows], gathered.at[dst, part, rows],
                r_send.at[index], r_recv.at[index], z_peer(1),
            )
        return remote(
            gathered.at[hop - 1, part, rows], gathered.at[hop, part, rows],
            l_send.at[index], l_recv.at[index], z_peer(NZ - 1),
        )

    def finish_attended(stage):
        for part in range(2):
            rows = slice(part * half, (part + 1) * half)
            total = jnp.zeros((half, HEAD_DIM), F32) if stage == 0 else squares[rows, :]
            for i in range(2):
                h = 2 * stage + i
                att = within[rows, head(h)] + contract(aq[rows, head(h)], state[h], 1, 0)
                total = total + att * att
                gathered[0, stage, rows, head(i)] = (att * gate[rows, head(h)]).astype(BF16)
            squares[rows, :] = total
            chunk = 2 * stage + part
            slot_send(chunk, 1, chunk, True).start()
            slot_send(chunk, 1, chunk, False).start()

    finish_state(0)
    finish_attended(0)
    finish_state(1)
    finish_attended(1)
    for group in range(ROWS // 128):
        tile = squares[group * 128 : (group + 1) * 128, :]
        ss_own[group : group + 1, :] = jnp.sum(tile.T, axis=0, keepdims=True)

    square_sends = []
    for step in range(1, NZ):
        copy = remote(
            ss_own, ss_all.at[step - 1], ss_send.at[step - 1], ss_recv.at[step - 1], z_peer(step)
        )
        copy.start()
        square_sends.append(copy)

    others = pl.ds(1, NZ - 1)

    def share_rows(step):
        return pl.ds(pl.multiple_of(c * 256 + b * 64 + lax.rem(a + step, NX) * 16, 16), 16)

    def group_rows(step):
        return pl.ds(pl.multiple_of(c * 256 + lax.rem(b + step, NX) * 64, 64), 64)

    def ring_starts(rows, peer, send_sem, recv_sem):
        piece = weight.at[others, rows(0)]
        up = remote(piece, piece, send_sem.at[0], recv_sem.at[0], peer(1))
        down = remote(piece, piece, send_sem.at[1], recv_sem.at[1], peer(NX - 1))
        up.start()
        down.start()
        return [up, down]

    def ring_forwards(rows, peer, send_sem, recv_sem, copies):
        copies[0].wait_recv()
        from_below = weight.at[others, rows(NX - 1), pl.ds(0, HALF)]
        up = remote(from_below, from_below, send_sem.at[2], recv_sem.at[2], peer(1))
        up.start()
        copies[1].wait_recv()
        from_above = weight.at[others, rows(1), pl.ds(HALF, HALF)]
        down = remote(from_above, from_above, send_sem.at[3], recv_sem.at[3], peer(NX - 1))
        down.start()
        return [up, down]


    def project(slot, row, count, fresh=False):
        rows = pl.ds(pl.multiple_of(row, 128), count)
        for n in range(OUT // 256):
            cols = slice(n * 256, (n + 1) * 256)
            term = contract(gathered[slot, 0, rows, :], weight[slot, 0:PAIR, cols], 1, 0)
            term = term + contract(gathered[slot, 1, rows, :], weight[slot, PAIR:FEAT, cols], 1, 0)
            if fresh:
                acc[rows, cols] = term
            else:
                acc[rows, cols] += term

    load_w.wait()
    for part in range(2):
        project(0, part * 256, 256, fresh=True)

    def pass_on(index, _):
        hop = lax.div(index, NCHUNK) + 1
        chunk = lax.rem(index, NCHUNK)
        slot_send(index, hop, chunk, True).wait_recv()
        slot_send(index + NCHUNK, hop + 1, chunk, True).start()
        slot_send(index, hop, chunk, False).wait_recv()
        slot_send(index + NCHUNK, hop + 1, chunk, False).start()
        return 0

    def pass_range(start, stop):
        lax.fori_loop(start, stop, pass_on, 0)

    for copy in weight_z:
        copy.wait_recv()
    ring_a = ring_starts(share_rows, a_peer, wa_send, wa_recv)
    pass_range(0, 1)
    ring_a2 = ring_forwards(share_rows, a_peer, wa_send, wa_recv, ring_a)
    pass_range(1, 2)
    for copy in ring_a2:
        copy.wait_recv()
    ring_b = ring_starts(group_rows, b_peer, wb_send, wb_recv)

    def to_sibling(step):
        piece = weight.at[others, group_rows(step)]
        copy = remote(piece, piece, ws_send.at[step], ws_recv.at[step], sibling)
        copy.start()
        return copy

    sibling_sends = [to_sibling(0)]
    pass_range(2, 5)
    ring_b2 = ring_forwards(group_rows, b_peer, wb_send, wb_recv, ring_b)
    sibling_sends.append(to_sibling(1))
    sibling_sends.append(to_sibling(3))
    pass_range(5, 8)
    for copy in ring_b2:
        copy.wait_recv()
    sibling_sends.append(to_sibling(2))
    for copy in sibling_sends:
        copy.wait_recv()

    def last_hop(unit, up):
        chunk = unit // 2
        rows = pl.ds((chunk % 2) * half + (unit % 2) * 128, 128)
        src, sends, recvs, device = (
            (5, r_send, r_recv, z_peer(1)) if up else (3, l_send, l_recv, z_peer(NZ - 1))
        )
        index = 3 * NCHUNK + unit
        return remote(
            gathered.at[src, chunk // 2, rows], gathered.at[4, chunk // 2, rows],
            sends.at[index], recvs.at[index], device,
        )

    def hop_three(chunk):
        index = 2 * NCHUNK + chunk
        units = (2 * chunk, 2 * chunk + 1)
        up = units[1] < NCHUNK
        slot_send(index, 3, chunk, True).wait_recv()
        if up:
            for unit in units:
                last_hop(unit, True).start()
        slot_send(index, 3, chunk, False).wait_recv()
        if not up:
            for unit in units:
                last_hop(unit, False).start()

    def project_whole(slot):
        def body(part, _):
            project(slot, part * 256, 256)
            return 0
        lax.fori_loop(0, 2, body, 0)

    hop_three(0)
    project_whole(7)
    hop_three(1)
    project_whole(1)
    hop_three(2)
    project_whole(6)
    hop_three(3)
    project_whole(2)
    project_whole(5)
    project_whole(3)

    for step in range(NZ - 1):
        square_sends[step].wait_recv()
    sums = ss_own[...]
    for step in range(NZ - 1):
        sums = sums + ss_all[step]
    factor = lax.rsqrt(sums / (HEADS * HEAD_DIM) + 1e-06)

    for group in range(ROWS // 128):
        last_hop(group, True).wait_recv()
        last_hop(group + NCHUNK, False).wait_recv()
        project(4, group * 128, 128)
        rows = slice(group * 128, (group + 1) * 128)
        column = jnp.broadcast_to(factor[group : group + 1, :], (128, 128)).T
        for n in range(OUT // 128):
            cols = slice(n * 128, (n + 1) * 128)
            out_ref[rows, cols] = (acc[rows, cols] * column).astype(BF16)

    @pl.when(c == 0)
    def _():
        for h in range(4):
            to_core1(h).wait_send()

    @pl.when(c == 1)
    def _():
        for stage in range(2):
            to_core0(stage).wait_send()
        for h in range(4):
            for step in range(1, NX):
                pl.when(first_sends(h, step))(first_phase(h, step).wait_send)
                pl.when(second_sends(h, step))(second_phase(h, step).wait_send)

    for copy in (
        weight_z + square_sends + ring_a + ring_a2 + ring_b + ring_b2 + sibling_sends
    ):
        copy.wait_send()

    def drain(index, _):
        hop = lax.div(index, NCHUNK) + 1
        chunk = lax.rem(index, NCHUNK)
        slot_send(index, hop, chunk, True).wait_send()
        slot_send(index, hop, chunk, False).wait_send()
        return 0

    lax.fori_loop(0, 3 * NCHUNK, drain, 0)
    for unit in range(2 * NCHUNK):
        last_hop(unit, unit < NCHUNK).wait_send()


def body(*arrays):
    dma = pltpu.SemaphoreType.DMA
    full = (4, HEAD_DIM, HEAD_DIM)
    vmem = pltpu.VMEM
    return pl.pallas_call(
        kernel,
        out_shape=jax.ShapeDtypeStruct((ROWS, OUT), BF16),
        in_specs=[pl.BlockSpec(memory_space=pl.ANY)] * 5,
        out_specs=pl.BlockSpec(memory_space=pltpu.VMEM),
        scratch_shapes=[
            vmem((ROWS, FEAT), BF16), vmem((ROWS, FEAT), BF16),
            vmem((ROWS, FEAT), BF16), vmem((ROWS, FEAT), BF16),
            vmem((ROWS, FEAT), BF16), vmem((ROWS, FEAT), BF16), vmem((ROWS, FEAT), BF16),
            vmem((ROWS, FEAT), F32), vmem((ROWS, FEAT), F32), vmem((ROWS, HEAD_DIM), F32),
            vmem(full, F32), vmem(full, BF16), vmem(full, BF16), vmem(full, BF16), vmem(full, F32),
            vmem((4, NX - 1, HEAD_DIM, HEAD_DIM), BF16), vmem((4, 2, HEAD_DIM, HEAD_DIM), BF16),
            vmem((4, NX - 1, HEAD_DIM, HEAD_DIM), BF16), vmem(full, BF16), vmem(full, BF16),
            vmem((NZ, 2, ROWS, PAIR), BF16), vmem((NZ, ROWS, OUT), BF16),
            vmem((ROWS, OUT), F32), vmem((4, 128), F32), vmem((NZ - 1, 4, 128), F32),
            pltpu.SemaphoreType.REGULAR((2,)), dma((7,)), dma((NZ - 1,)), dma((NZ - 1,)), dma((6,)), dma((6,)),
            dma((12,)), dma((12,)), dma((12,)), dma((12,)),
            dma((NZ - 1,)), dma((NZ - 1,)),
            dma((5 * NCHUNK,)), dma((5 * NCHUNK,)), dma((5 * NCHUNK,)), dma((5 * NCHUNK,)),
            dma((4,)), dma((4,)), dma((4,)), dma((4,)), dma((4,)), dma((4,)),
        ],
        compiler_params=pltpu.CompilerParams(
            collective_id=0, has_side_effects=True, vmem_limit_bytes=48 * 1024 * 1024
        ),
        cost_estimate=pl.CostEstimate(
            flops=3_900_000_000, bytes_accessed=9_000_000, transcendentals=1_000_000
        ),
    )(*(pltpu.with_memory_space_constraint(arg, pltpu.HBM) for arg in arrays))


def solution(mesh):
    return jax.shard_map(
        body,
        mesh=mesh,
        in_specs=(
            P("seq", "head"),
            P("seq", "head"),
            P("seq", "head"),
            P("seq", "head"),
            P("head", None),
        ),
        out_specs=P("seq", "head"),
        check_vma=False,
    )
```
